32 devices in a mesh: cells: 16 (over z, x, core), nets: 2 (over y).
Axes of the slice: x: 2, y: 2, z: 4, core: 2. Of those that a mesh axis runs over, the one named last changes fastest.
Arguments:
- grad_out: bfloat16 [32768, 512], P(('cells', 'nets')), may hold values from -6 to 6
- saved_agg: bfloat16 [32768, 512], P(('cells', 'nets')), may hold values from -0.03125 to 0.03125
- theta: bfloat16 [512, 512], replicated, may hold values from -0.25 to 0.25
- tile_values: bfloat16 [16, 2, 16, 128, 128], P('cells', 'nets'), may hold values from -0.5 to 0.5
- tile_coords: int32 [16, 2, 16, 2], P('cells', 'nets'), may hold values from 0 to 15, as said below
- block_tile_count: int32 [16, 2], P('cells', 'nets'), may hold values from 4 to 16, as said below
- cell_degree: int32 [32768], P('cells'), may hold values from 1 to 8
- net_pin_count: int32 [2048], P('nets'), may hold values from 12 to 39
Outputs:
- grad_cells: bfloat16 [32768, 512], P(('cells', 'nets'))
- layer_weight_gradient: bfloat16 [512, 512], replicated
The draws below stay inside these ranges and needn't reach their ends.
Inputs may be any that keep to these rules, and one draw needn't show every extreme that they name: `tile_coords`: within each block the 16 slots name distinct tiles: column 0 a cell tile below 16, column 1 a net tile below 8. Slots at and beyond the block's count carry no weight. `block_tile_count`: live slots of each block are its first ones; some block of every draw has all 16 live.
All inputs are finite; a program needn't handle non-finite values.
Results may differ from the reference program's by a relative error of at most 0.015.
Values may be sent and summed in bfloat16 or wider, within the bound.
A program may use at most 64 MiB of HBM per device.

```python
import jax
import jax.numpy as jnp
from jax import lax

D = 512
TILE = 128
CBLK = 2048
NBLK = 1024
TILES_DEV = 16
NC = 32768
NE = 2048
N_CELLS = 16
N_NETS = 2


def draw_tile_coords(key, part):
    net_tiles = NBLK // TILE
    slot_total = CBLK // TILE * net_tiles
    block_keys = jax.random.split(key, N_CELLS * N_NETS)
    chosen = jax.vmap(lambda block_key: jax.random.permutation(block_key, slot_total)[:TILES_DEV])(block_keys)
    chosen = chosen.astype(jnp.int32).reshape(N_CELLS, N_NETS, TILES_DEV)
    return jnp.stack([chosen // net_tiles, chosen % net_tiles], axis=-1).astype(jnp.int32)


def draw_block_tile_count(key, part):
    level = jax.random.randint(key, (N_CELLS * N_NETS,), 1, 5)
    counts = TILES_DEV // level
    chosen_block = jax.random.randint(jax.random.fold_in(key, 7), (), 0, N_CELLS * N_NETS)
    counts = jnp.where(jnp.arange(N_CELLS * N_NETS) == chosen_block, TILES_DEV, counts)
    return counts.reshape(N_CELLS, N_NETS).astype(jnp.int32)


def with_ends(result, rng, smallest, largest):
    shape = result.shape
    place = [jax.random.randint(jax.random.fold_in(rng, axis), (), 0, shape[axis]) for axis in range(len(shape))]
    result = result.at[tuple(place)].set(smallest)
    longest = shape.index(max(shape))
    place[longest] = (place[longest] + 1) % shape[longest]
    return result.at[tuple(place)].set(largest)


def block_scale(rng, dims, cuts, smallest, largest):
    def one(dim, blocks):
        steps = jax.random.uniform(jax.random.fold_in(jax.random.fold_in(rng, 6), dim), (blocks,), jnp.float32, smallest / len(cuts), largest / len(cuts))
        return jnp.repeat(jnp.exp(steps), dims[dim] // blocks).reshape((-1,) + (1,) * (len(dims) - dim - 1))

    loudness = one(*cuts[0])
    for cut in cuts[1:]:
        loudness = loudness * one(*cut)
    return loudness


def bell_draw(stream_key, extent, width, most, shards=(), held_as=jnp.bfloat16):
    drawn = jax.random.normal(stream_key, extent, jnp.float32) * width
    if len(shards) > 0:
        drawn = block_scale(stream_key, extent, shards, -0.22, 0.18) * drawn
    return jnp.clip(drawn, min=-most, max=most).astype(held_as)


def setup_inputs(seed: int = 0) -> dict:
    key_list = jax.random.split(jax.random.key(seed), 9)
    return {
        "grad_out": bell_draw(key_list[0], (NC, D), 1.0, 6.0, ((0, 32),)),
        "saved_agg": bell_draw(key_list[1], (NC, D), NC ** -0.5, 0.03125, ((0, 32),)),
        "theta": bell_draw(key_list[2], (D, D), D ** -0.5, 0.25),
        "tile_values": bell_draw(key_list[3], (N_CELLS, N_NETS, TILES_DEV, TILE, TILE), TILE ** -0.5, 0.5, ((0, 16), (1, 2))),
        "tile_coords": draw_tile_coords(jax.random.fold_in(key_list[8], 71), 0),
        "block_tile_count": draw_block_tile_count(jax.random.fold_in(key_list[8], 71), 0),
        "cell_degree": with_ends(jax.random.randint(key_list[6], (NC,), 1, 9), jax.random.fold_in(key_list[6], 1), 1, 8).astype(jnp.int32),
        "net_pin_count": with_ends(jax.random.randint(key_list[7], (NE,), 12, 40), jax.random.fold_in(key_list[7], 1), 12, 39).astype(jnp.int32),
    }


def dense_block(tile_vals, coords, live_count):
    cell_tiles = CBLK // TILE
    net_tiles = NBLK // TILE
    live_mask = jnp.arange(TILES_DEV, dtype=jnp.int32) < live_count
    row_pick = ((coords[:, 0:1] == jnp.arange(cell_tiles, dtype=jnp.int32)[None, :]) & live_mask[:, None]).astype(jnp.float32)
    col_pick = (coords[:, 1:2] == jnp.arange(net_tiles, dtype=jnp.int32)[None, :]).astype(jnp.float32)
    dense = jnp.einsum('tr,tc,tmk->rmck', row_pick, col_pick, tile_vals.astype(jnp.float32))
    return dense.reshape(CBLK, NBLK).astype(jnp.bfloat16)

def reference(grad_out, saved_agg, theta, tile_values, tile_coords, block_tile_count, cell_degree, net_pin_count):
    grad_z = jnp.dot(grad_out, theta.T, preferred_element_type=jnp.float32)
    cell_root = jnp.sqrt(cell_degree.astype(jnp.float32))[:, None]
    scaled = (grad_z / cell_root).astype(jnp.bfloat16).reshape(N_CELLS, CBLK, D)

    def net_step(running, inputs):
        block_entries_list, block_coords, block_counts, block_rows = inputs

        def one_block(tile_vals, coords, live_count):
            return jnp.dot(dense_block(tile_vals, coords, live_count).T, block_rows, preferred_element_type=jnp.float32)
        return (running + jax.vmap(one_block)(block_entries_list, block_coords, block_counts), None)
    net_sum, _ = lax.scan(net_step, jnp.zeros((N_NETS, NBLK, D), jnp.float32), (tile_values, tile_coords, block_tile_count, scaled))
    net_grad = (net_sum / net_pin_count.reshape(N_NETS, NBLK, 1).astype(jnp.float32)).astype(jnp.bfloat16)

    def cell_block(inputs):
        block_entries_list, block_coords, block_counts = inputs

        def one_block(tile_vals, coords, live_count, net_rows):
            return jnp.dot(dense_block(tile_vals, coords, live_count), net_rows, preferred_element_type=jnp.float32).astype(jnp.bfloat16)
        partials = jax.vmap(one_block)(block_entries_list, block_coords, block_counts, net_grad)
        return lax.optimization_barrier(jnp.sum(partials.astype(jnp.float32), axis=0))
    cell_sum = lax.map(cell_block, (tile_values, tile_coords, block_tile_count)).reshape(N_CELLS * CBLK, D)
    grad_cells = (cell_sum / cell_root).astype(jnp.bfloat16)
    layer_weight_gradient = jnp.dot(saved_agg.T, grad_out, preferred_element_type=jnp.float32).astype(jnp.bfloat16)
    return (grad_cells, layer_weight_gradient)
```

```python
import functools

import jax
import jax.numpy as jnp
from jax import lax
from jax.experimental import pallas as pl
from jax.experimental.pallas import tpu as pltpu
from jax.sharding import PartitionSpec as P

TBLK = 16
CHUNKS = 2
F32 = jnp.float32
BF16 = jnp.bfloat16
MESH = pl.DeviceIdType.MESH


def spread_nets(tile_vals, coords, live_mask, cell_tiles, net_count):
    tile_len = tile_vals.shape[-1]
    feature_dim = cell_tiles.shape[-1]
    running = jnp.zeros((net_count, tile_len, feature_dim), jnp.float32)
    selected_tiles = cell_tiles[coords[0:TBLK, 0]]
    matrix_product = jnp.einsum(
        "cnr,cnw->crw", tile_vals, selected_tiles, preferred_element_type=jnp.float32
    )
    weight = live_mask.astype(jnp.float32)[:, None, None]
    running = running.at[coords[0:TBLK, 1]].add(matrix_product * weight)
    return running


def spread_cells(tile_vals, coords, live_mask, net_tiles, number_of_cells):
    tile_len = tile_vals.shape[-1]
    feature_dim = net_tiles.shape[-1]
    running = jnp.zeros((number_of_cells, tile_len, feature_dim), jnp.float32)
    selected_tiles = net_tiles[coords[0:TBLK, 1]]
    matrix_product = jnp.einsum(
        "jaf,jfw->jaw", tile_vals, selected_tiles, preferred_element_type=jnp.float32
    )
    weight = live_mask.astype(jnp.float32)[:, None, None]
    running = running.at[coords[0:TBLK, 0]].add(matrix_product * weight)
    return running


def shards(
    grad_out,
    saved_agg,
    theta,
    tile_values,
    tile_coords,
    block_tile_count,
    cell_degree,
    net_pin_count,
):
    own_rows = grad_out.shape[0]
    feature_dim = grad_out.shape[1]
    net_position = lax.axis_index("nets")
    cell_position = lax.axis_index("cells")
    own_degree = lax.dynamic_slice_in_dim(cell_degree, net_position * own_rows, own_rows)
    own_root = jnp.sqrt(own_degree.astype(jnp.float32))[:, None]
    grad_z = lax.dot_general(
        grad_out, theta, (((1,), (1,)), ((), ())), preferred_element_type=jnp.float32
    )
    scaled = (grad_z / own_root).astype(jnp.bfloat16)
    gathered = lax.all_gather(scaled, "nets", axis=0, tiled=True)
    theta_term = lax.dot_general(
        saved_agg, grad_out, (((0,), (0,)), ((), ())), preferred_element_type=jnp.float32
    )
    layer_weight_gradient = lax.psum(theta_term, ("cells", "nets")).astype(jnp.bfloat16)
    tile_vals = tile_values[0, 0]
    coords = tile_coords[0, 0]
    live_mask = jnp.arange(tile_vals.shape[0], dtype=jnp.int32) < block_tile_count[0, 0]
    block_cells = gathered.shape[0]
    block_nets = net_pin_count.shape[0]
    tile_len = tile_vals.shape[-1]
    number_of_cells = block_cells // tile_len
    net_count = block_nets // tile_len
    cell_tiles = gathered.reshape(number_of_cells, tile_len, feature_dim)
    net_partial = spread_nets(tile_vals, coords, live_mask, cell_tiles, net_count).reshape(
        block_nets, feature_dim
    )
    net_share = lax.psum_scatter(net_partial, "cells", scatter_dimension=0, tiled=True)
    share_rows = net_share.shape[0]
    share_degree = lax.dynamic_slice_in_dim(net_pin_count, cell_position * share_rows, share_rows)
    gradient_share = (net_share / share_degree.astype(jnp.float32)[:, None]).astype(jnp.bfloat16)
    net_grad = lax.all_gather(gradient_share, "cells", axis=0, tiled=True)
    net_tiles = net_grad.reshape(net_count, tile_len, feature_dim)
    cell_partial = spread_cells(tile_vals, coords, live_mask, net_tiles, number_of_cells).reshape(
        block_cells, feature_dim
    )
    cell_total = lax.psum_scatter(
        cell_partial.astype(jnp.bfloat16), "nets", scatter_dimension=0, tiled=True
    ).astype(jnp.float32)
    grad_cells = (cell_total / own_root).astype(jnp.bfloat16)
    return (grad_cells, layer_weight_gradient)


def exchange_kernel(
    grad_out, saved_agg, theta, tile_values, inv_vec, inv_own, degree, pins,
    out_cells, out_weight,
    go, sa, th, tiles_own, tiles_far, inv_land, inv_far, inc, scaled,
    part, part_core, part_x, part_y, part_z, grads,
    wpart, wpart_core, wpart_x, wpart_y, wpart_z, wgrads,
    local_sem, send_sem, recv_sem,
):
    cell = lax.axis_index("cells")
    y = lax.axis_index("nets")
    z, x, core = cell // 4, (cell // 2) % 2, cell % 2

    def device(zt, xt, ct, yt):
        return ((zt * 2 + xt) * 2 + ct, yt)

    to_core = device(z, x, 1 - core, y)
    to_x = device(z, 1 - x, core, y)
    to_y = device(z, x, core, 1 - y)
    z_of = [lax.rem(z + d, 4) for d in range(4)]
    to_z = [device(z_of[d], x, core, y) for d in range(4)]

    loads = [
        pltpu.make_async_copy(src, dst, local_sem.at[i])
        for i, (src, dst) in enumerate(
            ((theta, th), (grad_out, go), (tile_values.at[0, 0], tiles_own.at[pl.ds(0, 16)]), (saved_agg, sa))
        )
    ]
    for load in loads:
        load.start()

    barrier = pltpu.get_barrier_semaphore()
    partners = [to_core, to_x, to_y, to_z[1], to_z[2], to_z[3]]
    for partner in partners:
        pl.semaphore_signal(barrier, inc=1, device_id=partner, device_id_type=MESH)
    pl.semaphore_wait(barrier, len(partners))

    copies = []

    def send(src, dst, target):
        i = len(copies)
        copy = pltpu.make_async_remote_copy(
            src_ref=src, dst_ref=dst, send_sem=send_sem.at[i], recv_sem=recv_sem.at[i],
            device_id=target, device_id_type=MESH,
        )
        copy.start()
        copies.append(copy)
        return copy

    inv_copy = send(inv_vec, inv_land, to_y)
    tile_copy = send(tile_values.at[0, 0], tiles_far.at[pl.ds(0, 16)], to_y)

    tile_len = tiles_own.shape[-1]
    zero_tile = jnp.zeros((tile_len, tile_len), BF16)
    tiles_own[16] = zero_tile
    tiles_far[16] = zero_tile

    def dense(tiles, inv, block):
        def row(r, carry):
            for j in range(8):
                slot = inv[0, (y * 8 + r) * 8 + j]
                inc[
                    block * 4 + j // 2,
                    pl.ds(pl.multiple_of(r * tile_len, tile_len), tile_len),
                    (j % 2) * tile_len : (j % 2 + 1) * tile_len,
                ] = tiles[slot]
            return carry

        lax.fori_loop(0, 8, row, 0)

    half = scaled.shape[1]
    row_len = part.shape[3]

    def net_part(h, block, xt):
        def pair(p, carry):
            j = block * 4 + xt * 2 + p
            product = jnp.dot(scaled[h], inc[j], preferred_element_type=F32).astype(BF16)
            for q in range(CHUNKS):
                for s in range(2):
                    part[q, h, j * 2 + s] = product[
                        q * row_len : (q + 1) * row_len, s * tile_len : (s + 1) * tile_len
                    ]
            return carry

        lax.fori_loop(0, 2, pair, 0)

    def add(a, b):
        return (a.astype(F32) + b.astype(F32)).astype(BF16)

    def piece(block, xt):
        return pl.ds(block * 8 + xt * 4, 4)

    main = [
        (part.at[q], part_core.at[q], part_x.at[q], part_y.at[q], part_z.at[q], grads.at[q])
        for q in range(CHUNKS)
    ]
    weight = (wpart, wpart_core, wpart_x, wpart_y, wpart_z, wgrads)

    def core_send(st, block, xt):
        return send(st[0].at[1 - core, piece(block, xt)], st[1].at[piece(block, xt)], to_core)

    def core_add(st, copy, block, xt):
        copy.wait_recv()
        at = piece(block, xt)
        st[0][core, at] = add(st[0][core, at], st[1][at])

    def x_send(st, block):
        return send(st[0].at[core, piece(block, 1 - x)], st[2].at[block], to_x)

    def x_add(st, copy, block):
        copy.wait_recv()
        at = piece(block, x)
        st[0][core, at] = add(st[0][core, at], st[2][block])

    def y_send(st):
        return send(st[0].at[core, piece(1 - y, x)], st[3], to_y)

    def y_add(st, copy):
        copy.wait_recv()
        at = piece(y, x)
        st[0][core, at] = add(st[0][core, at], st[3][...])

    mine = y * 8 + x * 4

    def z_send(st):
        return [send(st[0].at[core, mine + z_of[d]], st[4].at[d - 1], to_z[d]) for d in (1, 2, 3)]

    def z_total(st, zs):
        total = st[0][core, mine + z].astype(F32)
        for d in (1, 2, 3):
            zs[d - 1].wait_recv()
            total = total + st[4][d - 1].astype(F32)
        return total

    def z_back(st):
        at = st[5].at[core, mine + z]
        return [send(at, at, to_z[d]) for d in (1, 2, 3)]

    def forward(st, block, xt, target):
        at = st[5].at[core, piece(block, xt)]
        return send(at, at, target)

    loads[0].wait()
    loads[1].wait()
    cells = go.shape[0]
    root = jnp.sqrt(degree[0:1, pl.ds(pl.multiple_of(y * cells, cells), cells)].astype(F32))
    for i in range(4):
        n = cells // 4
        for h in range(2):
            z_rows = lax.dot_general(
                th[h * half : (h + 1) * half], go[i * n : (i + 1) * n], (((1,), (1,)), ((), ())),
                preferred_element_type=F32,
            )
            scaled[h, :, i * n : (i + 1) * n] = (z_rows / root[:, i * n : (i + 1) * n]).astype(BF16)

    loads[2].wait()
    dense(tiles_own, inv_own, y)
    first = {}
    for side in (0, 1):
        xt = 1 - x if side == 0 else x
        net_part(1 - core, y, xt)
        first[side] = [core_send(st, y, xt) for st in main]
        net_part(core, y, xt)
    x_own = []
    for q, st in enumerate(main):
        core_add(st, first[0][q], y, 1 - x)
        x_own.append(x_send(st, y))

    loads[3].wait()
    per = wpart.shape[2]

    def weight_rows(i, carry):
        rows = sa[:, pl.ds(pl.multiple_of(i * 128, 128), 128)]
        term = lax.dot_general(rows, go[...], (((0,), (0,)), ((), ())), preferred_element_type=F32)
        term = term.astype(BF16)
        for j in range(128 // per):
            wpart[i // 2, (i % 2) * (128 // per) + j] = term[j * per : (j + 1) * per]
        return carry

    lax.fori_loop(0, 4, weight_rows, 0)
    w_core = {}
    for block in (0, 1):
        for side in (0, 1):
            w_core[block, side] = core_send(weight, block, 1 - x if side == 0 else x)
    for q, st in enumerate(main):
        core_add(st, first[1][q], y, x)
    w_x = []
    for block in (0, 1):
        core_add(weight, w_core[block, 0], block, 1 - x)
        w_x.append(x_send(weight, block))
    for block in (0, 1):
        core_add(weight, w_core[block, 1], block, x)
    for q, st in enumerate(main):
        x_add(st, x_own[q], y)
    for block in (0, 1):
        x_add(weight, w_x[block], block)

    inv_copy.wait_recv()
    inv_move = pltpu.make_async_copy(inv_land, inv_far, local_sem.at[4])
    inv_move.start()
    inv_move.wait()
    tile_copy.wait_recv()
    w_y = y_send(weight)
    dense(tiles_far, inv_far, 1 - y)
    for side in (0, 1):
        xt = 1 - x if side == 0 else x
        net_part(1 - core, 1 - y, xt)
        first[side] = [core_send(st, 1 - y, xt) for st in main]
        net_part(core, 1 - y, xt)
    x_far = []
    for q, st in enumerate(main):
        core_add(st, first[0][q], 1 - y, 1 - x)
        x_far.append(x_send(st, 1 - y))
    for q, st in enumerate(main):
        core_add(st, first[1][q], 1 - y, x)
    y_add(weight, w_y)
    w_z = z_send(weight)
    ys = []
    for q, st in enumerate(main):
        x_add(st, x_far[q], 1 - y)
        ys.append(y_send(st))
    weight[5][core, mine + z] = z_total(weight, w_z).astype(BF16)
    w_zb = z_back(weight)
    zs = []
    for q, st in enumerate(main):
        y_add(st, ys[q])
        zs.append(z_send(st))
    for copy in w_zb:
        copy.wait_recv()
    w_yb = forward(weight, y, x, to_y)
    w_xb = [forward(weight, y, x, to_x)]
    w_cb = [forward(weight, y, x, to_core)]
    pin_row = pins[0:1, pl.ds(pl.multiple_of((x * 4 + z) * tile_len, tile_len), tile_len)].astype(F32)
    zb = []
    for q, st in enumerate(main):
        st[5][core, mine + z] = (z_total(st, zs[q]) / pin_row).astype(BF16)
        zb.append(z_back(st))
    w_yb.wait_recv()
    w_xb.append(forward(weight, 1 - y, x, to_x))
    w_cb.append(forward(weight, 1 - y, x, to_core))
    yb, xb, cb = [], [], []
    for q, st in enumerate(main):
        for copy in zb[q]:
            copy.wait_recv()
        yb.append(forward(st, y, x, to_y))
        xb.append([forward(st, y, x, to_x)])
        cb.append(forward(st, y, x, to_core))
    for i in (0, 1):
        w_xb[i].wait_recv()
        w_cb.append(forward(weight, y if i == 0 else 1 - y, 1 - x, to_core))
    for q, st in enumerate(main):
        yb[q].wait_recv()
        xb[q].append(forward(st, 1 - y, x, to_x))
        cb.append(forward(st, 1 - y, x, to_core))
    for copy in w_cb:
        copy.wait_recv()
    for t in range(32):
        out_weight[t * per : (t + 1) * per, :] = wgrads[t // 16, t % 16]
    for i in (0, 1):
        for q, st in enumerate(main):
            xb[q][i].wait_recv()
            cb.append(forward(st, y if i == 0 else 1 - y, 1 - x, to_core))
    for copy in cb:
        copy.wait_recv()

    def cell_rows(r, carry):
        at = pl.ds(pl.multiple_of(r * 128, 128), 128)
        root_row = jnp.sqrt(
            degree[0:1, pl.ds(pl.multiple_of(y * cells + r * 128, 128), 128)].astype(F32)
        )
        root_tile = jnp.broadcast_to(root_row, (128, 128)).T
        for h in range(2):
            for q in range(CHUNKS):
                total = jnp.zeros((128, row_len), F32)
                for j in range(8):
                    net_rows = jnp.concatenate([grads[q, h, 2 * j], grads[q, h, 2 * j + 1]], axis=1)
                    total = total + lax.dot_general(
                        inc[j, at, :], net_rows, (((1,), (1,)), ((), ())), preferred_element_type=F32
                    )
                at_col = h * half + q * row_len
                out_cells[at, at_col : at_col + row_len] = (total / root_tile[:, :row_len]).astype(BF16)
        return carry

    lax.fori_loop(0, cells // 128, cell_rows, 0)
    for copy in copies:
        copy.wait_send()


def fused_shards(
    grad_out, saved_agg, theta, tile_values, tile_coords, block_tile_count, cell_degree, net_pin_count
):
    rows, width = grad_out.shape
    slots, tile_len = tile_values.shape[2], tile_values.shape[3]
    nets = net_pin_count.shape[0]
    net_tiles = nets // tile_len
    places = jnp.arange(128, dtype=jnp.int32)
    coords = tile_coords[0, 0]
    slot = jnp.arange(slots, dtype=jnp.int32)
    code = jnp.where(slot < block_tile_count[0, 0], coords[:, 0] * net_tiles + coords[:, 1], -1)
    found = code[:, None] == places[None, :]
    inv = slots + jnp.sum(jnp.where(found, slot[:, None] - slots, 0), axis=0)
    inv = jnp.broadcast_to(inv[None, :], (8, 128)).astype(jnp.int32)
    half, row_len = width // 2, width // 2 // CHUNKS
    per = width // 32
    vmem = pltpu.VMEM
    any_spec = pl.BlockSpec(memory_space=pl.ANY)
    vmem_spec = pl.BlockSpec(memory_space=pltpu.VMEM)

    def stage_buffers(lead, block):
        return [
            vmem(lead + (2, 16) + block, BF16),
            vmem(lead + (16,) + block, BF16),
            vmem(lead + (2, 4) + block, BF16),
            vmem(lead + (4,) + block, BF16),
            vmem(lead + (3,) + block, BF16),
            vmem(lead + (2, 16) + block, BF16),
        ]

    return pl.pallas_call(
        exchange_kernel,
        out_shape=(
            jax.ShapeDtypeStruct((rows, width), BF16),
            jax.ShapeDtypeStruct((width, width), BF16),
        ),
        in_specs=[any_spec] * 4
        + [vmem_spec, pl.BlockSpec(memory_space=pltpu.SMEM), vmem_spec, vmem_spec],
        out_specs=(vmem_spec, vmem_spec),
        scratch_shapes=[
            vmem((rows, width), BF16),
            vmem((rows, width), BF16),
            vmem((width, width), BF16),
            vmem((slots + 1, tile_len, tile_len), BF16),
            vmem((slots + 1, tile_len, tile_len), BF16),
            vmem((8, 128), jnp.int32),
            pltpu.SMEM((8, 128), jnp.int32),
            vmem((net_tiles, rows, 2 * tile_len), BF16),
            vmem((2, half, rows), BF16),
        ]
        + stage_buffers((CHUNKS,), (row_len, tile_len))
        + stage_buffers((), (per, width))
        + [
            pltpu.SemaphoreType.DMA((8,)),
            pltpu.SemaphoreType.DMA((96,)),
            pltpu.SemaphoreType.DMA((96,)),
        ],
        compiler_params=pltpu.CompilerParams(
            collective_id=0, has_side_effects=True, vmem_limit_bytes=48 * 1024 * 1024
        ),
    )(
        grad_out, saved_agg, theta, tile_values, inv, inv,
        cell_degree.reshape(1, -1), net_pin_count.reshape(1, -1),
    )


def solution(mesh):
    in_specs = (
        P(("cells", "nets"), None),
        P(("cells", "nets"), None),
        P(),
        P("cells", "nets", None, None, None),
        P("cells", "nets", None, None),
        P("cells", "nets"),
        P("cells"),
        P("nets"),
    )
    fused = mesh.shape["cells"] == 16 and mesh.shape["nets"] == 2
    out_specs = (P(("cells", "nets"), None), P())
    return jax.shard_map(
        fused_shards if fused else shards, mesh=mesh, in_specs=in_specs, out_specs=out_specs, check_vma=False,
    )
```

```python
import functools

import jax
import jax.numpy as jnp
from jax import lax
from jax.experimental import pallas as pl
from jax.experimental.pallas import tpu as pltpu
from jax.sharding import PartitionSpec as P

TBLK = 16
CHUNKS = 4
F32 = jnp.float32
BF16 = jnp.bfloat16
MESH = pl.DeviceIdType.MESH


def spread_nets(tile_vals, coords, live_mask, cell_tiles, net_count):
    tile_len = tile_vals.shape[-1]
    feature_dim = cell_tiles.shape[-1]
    running = jnp.zeros((net_count, tile_len, feature_dim), jnp.float32)
    selected_tiles = cell_tiles[coords[0:TBLK, 0]]
    matrix_product = jnp.einsum(
        "cnr,cnw->crw", tile_vals, selected_tiles, preferred_element_type=jnp.float32
    )
    weight = live_mask.astype(jnp.float32)[:, None, None]
    running = running.at[coords[0:TBLK, 1]].add(matrix_product * weight)
    return running


def spread_cells(tile_vals, coords, live_mask, net_tiles, number_of_cells):
    tile_len = tile_vals.shape[-1]
    feature_dim = net_tiles.shape[-1]
    running = jnp.zeros((number_of_cells, tile_len, feature_dim), jnp.float32)
    selected_tiles = net_tiles[coords[0:TBLK, 1]]
    matrix_product = jnp.einsum(
        "jaf,jfw->jaw", tile_vals, selected_tiles, preferred_element_type=jnp.float32
    )
    weight = live_mask.astype(jnp.float32)[:, None, None]
    running = running.at[coords[0:TBLK, 0]].add(matrix_product * weight)
    return running


def shards(
    grad_out,
    saved_agg,
    theta,
    tile_values,
    tile_coords,
    block_tile_count,
    cell_degree,
    net_pin_count,
):
    own_rows = grad_out.shape[0]
    feature_dim = grad_out.shape[1]
    net_position = lax.axis_index("nets")
    cell_position = lax.axis_index("cells")
    own_degree = lax.dynamic_slice_in_dim(cell_degree, net_position * own_rows, own_rows)
    own_root = jnp.sqrt(own_degree.astype(jnp.float32))[:, None]
    grad_z = lax.dot_general(
        grad_out, theta, (((1,), (1,)), ((), ())), preferred_element_type=jnp.float32
    )
    scaled = (grad_z / own_root).astype(jnp.bfloat16)
    gathered = lax.all_gather(scaled, "nets", axis=0, tiled=True)
    theta_term = lax.dot_general(
        saved_agg, grad_out, (((0,), (0,)), ((), ())), preferred_element_type=jnp.float32
    )
    layer_weight_gradient = lax.psum(theta_term, ("cells", "nets")).astype(jnp.bfloat16)
    tile_vals = tile_values[0, 0]
    coords = tile_coords[0, 0]
    live_mask = jnp.arange(tile_vals.shape[0], dtype=jnp.int32) < block_tile_count[0, 0]
    block_cells = gathered.shape[0]
    block_nets = net_pin_count.shape[0]
    tile_len = tile_vals.shape[-1]
    number_of_cells = block_cells // tile_len
    net_count = block_nets // tile_len
    cell_tiles = gathered.reshape(number_of_cells, tile_len, feature_dim)
    net_partial = spread_nets(tile_vals, coords, live_mask, cell_tiles, net_count).reshape(
        block_nets, feature_dim
    )
    net_share = lax.psum_scatter(net_partial, "cells", scatter_dimension=0, tiled=True)
    share_rows = net_share.shape[0]
    share_degree = lax.dynamic_slice_in_dim(net_pin_count, cell_position * share_rows, share_rows)
    gradient_share = (net_share / share_degree.astype(jnp.float32)[:, None]).astype(jnp.bfloat16)
    net_grad = lax.all_gather(gradient_share, "cells", axis=0, tiled=True)
    net_tiles = net_grad.reshape(net_count, tile_len, feature_dim)
    cell_partial = spread_cells(tile_vals, coords, live_mask, net_tiles, number_of_cells).reshape(
        block_cells, feature_dim
    )
    cell_total = lax.psum_scatter(
        cell_partial.astype(jnp.bfloat16), "nets", scatter_dimension=0, tiled=True
    ).astype(jnp.float32)
    grad_cells = (cell_total / own_root).astype(jnp.bfloat16)
    return (grad_cells, layer_weight_gradient)


def exchange_kernel(
    grad_out, saved_agg, theta, tile_values, coords, live, degree, pins,
    out_cells, out_weight,
    go, sa, th, tiles_own, tiles_far, inv_vec, inv_land, inv_own, inv_far, inc, scaled, cells_sum,
    part, part_core, part_x, part_y, part_z, grads,
    wpart, wpart_core, wpart_x, wpart_y, wpart_z, wgrads,
    local_sem, send_sem, recv_sem,
):
    cell = lax.axis_index("cells")
    y = lax.axis_index("nets")
    z, x, core = cell // 4, (cell // 2) % 2, cell % 2

    def device(zt, xt, ct, yt):
        return ((zt * 2 + xt) * 2 + ct, yt)

    to_core = device(z, x, 1 - core, y)
    to_x = device(z, 1 - x, core, y)
    to_y = device(z, x, core, 1 - y)
    z_of = [lax.rem(z + d, 4) for d in range(4)]
    to_z = [device(z_of[d], x, core, y) for d in range(4)]

    loads = [
        pltpu.make_async_copy(src, dst, local_sem.at[i])
        for i, (src, dst) in enumerate(
            ((theta, th), (grad_out, go), (tile_values.at[0, 0], tiles_own.at[pl.ds(0, 16)]), (saved_agg, sa))
        )
    ]
    for load in loads:
        load.start()

    barrier = pltpu.get_barrier_semaphore()
    partners = [to_core, to_x, to_y, to_z[1], to_z[2], to_z[3]]
    for partner in partners:
        pl.semaphore_signal(barrier, inc=1, device_id=partner, device_id_type=MESH)
    pl.semaphore_wait(barrier, len(partners))

    copies = []

    def send(src, dst, target):
        i = len(copies)
        copy = pltpu.make_async_remote_copy(
            src_ref=src, dst_ref=dst, send_sem=send_sem.at[i], recv_sem=recv_sem.at[i],
            device_id=target, device_id_type=MESH,
        )
        copy.start()
        copies.append(copy)
        return copy

    tile_copy = send(tile_values.at[0, 0], tiles_far.at[pl.ds(0, 16)], to_y)
    place = lax.broadcasted_iota(jnp.int32, (8, 128), 1)
    slots = jnp.full((8, 128), 16, jnp.int32)
    for t in range(16):
        code = coords[0, 0, 0, t] * 8 + coords[0, 0, 1, t]
        code = jnp.where(t < live[0, 0], code, -1)
        slots = jnp.where(place == code, t, slots)
    inv_vec[...] = slots
    inv_copy = send(inv_vec, inv_land, to_y)
    own_move = pltpu.make_async_copy(inv_vec, inv_own, local_sem.at[5])
    own_move.start()

    tile_len = tiles_own.shape[-1]
    zero_tile = jnp.zeros((tile_len, tile_len), BF16)
    tiles_own[16] = zero_tile
    tiles_far[16] = zero_tile

    def dense(tiles, inv, block):
        def row(r, carry):
            for j in range(8):
                slot = inv[0, (y * 8 + r) * 8 + j]
                inc[
                    block * 4 + j // 2,
                    pl.ds(pl.multiple_of(r * tile_len, tile_len), tile_len),
                    (j % 2) * tile_len : (j % 2 + 1) * tile_len,
                ] = tiles[slot]
            return carry

        lax.fori_loop(0, 8, row, 0)

    half = scaled.shape[1]
    row_len = part.shape[3]

    def net_part(h, block, xt):
        def pair(p, carry):
            j = block * 4 + xt * 2 + p
            product = jnp.dot(scaled[h], inc[j], preferred_element_type=F32).astype(BF16)
            for q in range(CHUNKS):
                for s in range(2):
                    part[q, h, j * 2 + s] = product[
                        q * row_len : (q + 1) * row_len, s * tile_len : (s + 1) * tile_len
                    ]
            return carry

        lax.fori_loop(0, 2, pair, 0)

    def add(a, b):
        return (a.astype(F32) + b.astype(F32)).astype(BF16)

    def piece(block, xt):
        return pl.ds(block * 8 + xt * 4, 4)

    main = [
        (part.at[q], part_core.at[q], part_x.at[q], part_y.at[q], part_z.at[q], grads.at[q])
        for q in range(CHUNKS)
    ]
    weight = (wpart, wpart_core, wpart_x, wpart_y, wpart_z, wgrads)

    def core_send(st, block, xt):
        return send(st[0].at[1 - core, piece(block, xt)], st[1].at[piece(block, xt)], to_core)

    def core_add(st, copy, block, xt):
        copy.wait_recv()
        at = piece(block, xt)
        st[0][core, at] = add(st[0][core, at], st[1][at])

    def x_send(st, block):
        return send(st[0].at[core, piece(block, 1 - x)], st[2].at[block], to_x)

    def x_add(st, copy, block):
        copy.wait_recv()
        at = piece(block, x)
        st[0][core, at] = add(st[0][core, at], st[2][block])

    def y_send(st):
        return send(st[0].at[core, piece(1 - y, x)], st[3], to_y)

    def y_add(st, copy):
        copy.wait_recv()
        at = piece(y, x)
        st[0][core, at] = add(st[0][core, at], st[3][...])

    mine = y * 8 + x * 4

    def z_send(st):
        return [send(st[0].at[core, mine + z_of[d]], st[4].at[d - 1], to_z[d]) for d in (1, 2, 3)]

    def z_total(st, zs):
        total = st[0][core, mine + z].astype(F32)
        for d in (1, 2, 3):
            zs[d - 1].wait_recv()
            total = total + st[4][d - 1].astype(F32)
        return total

    def z_back(st):
        at = st[5].at[core, mine + z]
        return [send(at, at, to_z[d]) for d in (1, 2, 3)]

    def forward(st, block, xt, target):
        at = st[5].at[core, piece(block, xt)]
        return send(at, at, target)

    loads[0].wait()
    loads[1].wait()
    cells = go.shape[0]
    root = jnp.sqrt(degree[0:1, pl.ds(pl.multiple_of(y * cells, cells), cells)].astype(F32))
    for i in range(4):
        n = cells // 4
        for h in range(2):
            z_rows = lax.dot_general(
                th[h * half : (h + 1) * half], go[i * n : (i + 1) * n], (((1,), (1,)), ((), ())),
                preferred_element_type=F32,
            )
            scaled[h, :, i * n : (i + 1) * n] = (z_rows / root[:, i * n : (i + 1) * n]).astype(BF16)

    loads[2].wait()
    own_move.wait()
    dense(tiles_own, inv_own, y)
    first = {}
    for side in (0, 1):
        xt = 1 - x if side == 0 else x
        net_part(1 - core, y, xt)
        first[side] = [core_send(st, y, xt) for st in main]
        net_part(core, y, xt)
    x_own = []
    for q, st in enumerate(main):
        core_add(st, first[0][q], y, 1 - x)
        x_own.append(x_send(st, y))

    loads[3].wait()
    per = wpart.shape[2]

    def weight_rows(i, carry):
        rows = sa[:, pl.ds(pl.multiple_of(i * 128, 128), 128)]
        term = lax.dot_general(rows, go[...], (((0,), (0,)), ((), ())), preferred_element_type=F32)
        term = term.astype(BF16)
        for j in range(128 // per):
            wpart[i // 2, (i % 2) * (128 // per) + j] = term[j * per : (j + 1) * per]
        return carry

    lax.fori_loop(0, 4, weight_rows, 0)
    w_core = {}
    for block in (0, 1):
        for side in (0, 1):
            w_core[block, side] = core_send(weight, block, 1 - x if side == 0 else x)
    for q, st in enumerate(main):
        core_add(st, first[1][q], y, x)
    w_x = []
    for block in (0, 1):
        core_add(weight, w_core[block, 0], block, 1 - x)
        w_x.append(x_send(weight, block))
    for block in (0, 1):
        core_add(weight, w_core[block, 1], block, x)
    for q, st in enumerate(main):
        x_add(st, x_own[q], y)
    for block in (0, 1):
        x_add(weight, w_x[block], block)

    inv_copy.wait_recv()
    inv_move = pltpu.make_async_copy(inv_land, inv_far, local_sem.at[4])
    inv_move.start()
    inv_move.wait()
    tile_copy.wait_recv()
    w_y = y_send(weight)
    dense(tiles_far, inv_far, 1 - y)
    for side in (0, 1):
        xt = 1 - x if side == 0 else x
        net_part(1 - core, 1 - y, xt)
        first[side] = [core_send(st, 1 - y, xt) for st in main]
        net_part(core, 1 - y, xt)
    x_far = []
    for q, st in enumerate(main):
        core_add(st, first[0][q], 1 - y, 1 - x)
        x_far.append(x_send(st, 1 - y))
    for q, st in enumerate(main):
        core_add(st, first[1][q], 1 - y, x)
    y_add(weight, w_y)
    w_z = z_send(weight)
    ys = []
    for q, st in enumerate(main):
        x_add(st, x_far[q], 1 - y)
        ys.append(y_send(st))
    weight[5][core, mine + z] = z_total(weight, w_z).astype(BF16)
    w_zb = z_back(weight)
    zs = []
    for q, st in enumerate(main):
        y_add(st, ys[q])
        zs.append(z_send(st))
    for copy in w_zb:
        copy.wait_recv()
    w_yb = forward(weight, y, x, to_y)
    w_xb = [forward(weight, y, x, to_x)]
    w_cb = [forward(weight, y, x, to_core)]
    pin_row = pins[0:1, pl.ds(pl.multiple_of((x * 4 + z) * tile_len, tile_len), tile_len)].astype(F32)
    zb = []
    for q, st in enumerate(main):
        st[5][core, mine + z] = (z_total(st, zs[q]) / pin_row).astype(BF16)
        zb.append(z_back(st))
    row_block = 256

    def cell_sum(h, pieces, start=False, last=False):
        def rows(r, carry):
            at = pl.ds(pl.multiple_of(r * row_block, row_block), row_block)
            total = None if start else cells_sum[h, at, :]
            for block, xt in pieces:
                for p in range(2):
                    j = block * 4 + xt * 2 + p
                    net_rows = jnp.concatenate(
                        [
                            jnp.concatenate([grads[q, h, 2 * j], grads[q, h, 2 * j + 1]], axis=1)
                            for q in range(CHUNKS)
                        ],
                        axis=0,
                    )
                    term = lax.dot_general(
                        inc[j, at, :], net_rows, (((1,), (1,)), ((), ())), preferred_element_type=F32
                    )
                    total = term if total is None else total + term
            if not last:
                cells_sum[h, at, :] = total
                return carry
            for i in range(row_block // 128):
                first_row = y * cells + r * row_block + i * 128
                root_row = jnp.sqrt(
                    degree[0:1, pl.ds(pl.multiple_of(first_row, 128), 128)].astype(F32)
                )
                root_tile = jnp.broadcast_to(root_row, (128, 128)).T
                out_at = pl.ds(pl.multiple_of(r * row_block + i * 128, 128), 128)
                for w in range(half // 128):
                    out_cells[out_at, pl.ds(pl.multiple_of(h * half + w * 128, 128), 128)] = (
                        total[i * 128 : (i + 1) * 128, w * 128 : (w + 1) * 128] / root_tile
                    ).astype(BF16)
            return carry

        lax.fori_loop(0, cells // row_block, rows, 0)

    yb, xb, cb = [], [], []
    for q, st in enumerate(main):
        for copy in zb[q]:
            copy.wait_recv()
        yb.append(forward(st, y, x, to_y))
        xb.append(forward(st, y, x, to_x))
        cb.append([forward(st, y, x, to_core)])
    w_yb.wait_recv()
    w_xb.append(forward(weight, 1 - y, x, to_x))
    w_cb.append(forward(weight, 1 - y, x, to_core))
    cell_sum(core, [(y, x)], start=True)
    diagonal = []
    for q, st in enumerate(main):
        yb[q].wait_recv()
        if q % 2 == 0:
            diagonal.append(forward(st, 1 - y, x, to_x))
        xb[q].wait_recv()
        if q % 2 == 1:
            diagonal.append(forward(st, y, 1 - x, to_y))
        cb[q].append(forward(st, 1 - y, x, to_core))
        cb[q].append(forward(st, y, 1 - x, to_core))
    for i in (0, 1):
        w_xb[i].wait_recv()
        w_cb.append(forward(weight, y if i == 0 else 1 - y, 1 - x, to_core))
    for q in range(CHUNKS):
        cb[q][0].wait_recv()
    cell_sum(1 - core, [(y, x)], start=True)
    cell_sum(core, [(1 - y, x), (y, 1 - x)])
    for q, st in enumerate(main):
        diagonal[q].wait_recv()
        cb[q].append(forward(st, 1 - y, 1 - x, to_core))
    for q in range(CHUNKS):
        cb[q][1].wait_recv()
        cb[q][2].wait_recv()
    cell_sum(1 - core, [(1 - y, x), (y, 1 - x)])
    cell_sum(core, [(1 - y, 1 - x)], last=True)
    for copy in w_cb:
        copy.wait_recv()
    for t in range(32):
        out_weight[t * per : (t + 1) * per, :] = wgrads[t // 16, t % 16]
    for q in range(CHUNKS):
        cb[q][3].wait_recv()
    cell_sum(1 - core, [(1 - y, 1 - x)], last=True)
    for copy in copies:
        copy.wait_send()


def fused_shards(
    grad_out, saved_agg, theta, tile_values, tile_coords, block_tile_count, cell_degree, net_pin_count
):
    rows, width = grad_out.shape
    slots, tile_len = tile_values.shape[2], tile_values.shape[3]
    nets = net_pin_count.shape[0]
    net_tiles = nets // tile_len
    half, row_len = width // 2, width // 2 // CHUNKS
    per = width // 32
    vmem = pltpu.VMEM
    any_spec = pl.BlockSpec(memory_space=pl.ANY)
    vmem_spec = pl.BlockSpec(memory_space=pltpu.VMEM)

    def stage_buffers(lead, block):
        return [
            vmem(lead + (2, 16) + block, BF16),
            vmem(lead + (16,) + block, BF16),
            vmem(lead + (2, 4) + block, BF16),
            vmem(lead + (4,) + block, BF16),
            vmem(lead + (3,) + block, BF16),
            vmem(lead + (2, 16) + block, BF16),
        ]

    return pl.pallas_call(
        exchange_kernel,
        out_shape=(
            jax.ShapeDtypeStruct((rows, width), BF16),
            jax.ShapeDtypeStruct((width, width), BF16),
        ),
        in_specs=[any_spec] * 4
        + [pl.BlockSpec(memory_space=pltpu.SMEM)] * 2 + [vmem_spec] * 2,
        out_specs=(vmem_spec, vmem_spec),
        scratch_shapes=[
            vmem((rows, width), BF16),
            vmem((rows, width), BF16),
            vmem((width, width), BF16),
            vmem((slots + 1, tile_len, tile_len), BF16),
            vmem((slots + 1, tile_len, tile_len), BF16),
            vmem((8, 128), jnp.int32),
            vmem((8, 128), jnp.int32),
            pltpu.SMEM((8, 128), jnp.int32),
            pltpu.SMEM((8, 128), jnp.int32),
            vmem((net_tiles, rows, 2 * tile_len), BF16),
            vmem((2, half, rows), BF16),
            vmem((2, rows, half), F32),
        ]
        + stage_buffers((CHUNKS,), (row_len, tile_len))
        + stage_buffers((), (per, width))
        + [
            pltpu.SemaphoreType.DMA((8,)),
            pltpu.SemaphoreType.DMA((160,)),
            pltpu.SemaphoreType.DMA((160,)),
        ],
        compiler_params=pltpu.CompilerParams(
            collective_id=0, has_side_effects=True, vmem_limit_bytes=60 * 1024 * 1024
        ),
    )(
        grad_out, saved_agg, theta, tile_values, jnp.swapaxes(tile_coords, 2, 3), block_tile_count,
        cell_degree.reshape(1, -1), net_pin_count.reshape(1, -1),
    )


def solution(mesh):
    in_specs = (
        P(("cells", "nets"), None),
        P(("cells", "nets"), None),
        P(),
        P("cells", "nets", None, None, None),
        P("cells", "nets", None, None),
        P("cells", "nets"),
        P("cells"),
        P("nets"),
    )
    fused = mesh.shape["cells"] == 16 and mesh.shape["nets"] == 2
    out_specs = (P(("cells", "nets"), None), P())
    return jax.shard_map(
        fused_shards if fused else shards, mesh=mesh, in_specs=in_specs, out_specs=out_specs, check_vma=False,
    )
```

```python
import functools

import jax
import jax.numpy as jnp
from jax import lax
from jax.experimental import pallas as pl
from jax.experimental.pallas import tpu as pltpu
from jax.sharding import PartitionSpec as P

TBLK = 16
CHUNKS = 4
F32 = jnp.float32
BF16 = jnp.bfloat16
MESH = pl.DeviceIdType.MESH


def spread_nets(tile_vals, coords, live_mask, cell_tiles, net_count):
    tile_len = tile_vals.shape[-1]
    feature_dim = cell_tiles.shape[-1]
    running = jnp.zeros((net_count, tile_len, feature_dim), jnp.float32)
    selected_tiles = cell_tiles[coords[0:TBLK, 0]]
    matrix_product = jnp.einsum(
        "cnr,cnw->crw", tile_vals, selected_tiles, preferred_element_type=jnp.float32
    )
    weight = live_mask.astype(jnp.float32)[:, None, None]
    running = running.at[coords[0:TBLK, 1]].add(matrix_product * weight)
    return running


def spread_cells(tile_vals, coords, live_mask, net_tiles, number_of_cells):
    tile_len = tile_vals.shape[-1]
    feature_dim = net_tiles.shape[-1]
    running = jnp.zeros((number_of_cells, tile_len, feature_dim), jnp.float32)
    selected_tiles = net_tiles[coords[0:TBLK, 1]]
    matrix_product = jnp.einsum(
        "jaf,jfw->jaw", tile_vals, selected_tiles, preferred_element_type=jnp.float32
    )
    weight = live_mask.astype(jnp.float32)[:, None, None]
    running = running.at[coords[0:TBLK, 0]].add(matrix_product * weight)
    return running


def shards(
    grad_out,
    saved_agg,
    theta,
    tile_values,
    tile_coords,
    block_tile_count,
    cell_degree,
    net_pin_count,
):
    own_rows = grad_out.shape[0]
    feature_dim = grad_out.shape[1]
    net_position = lax.axis_index("nets")
    cell_position = lax.axis_index("cells")
    own_degree = lax.dynamic_slice_in_dim(cell_degree, net_position * own_rows, own_rows)
    own_root = jnp.sqrt(own_degree.astype(jnp.float32))[:, None]
    grad_z = lax.dot_general(
        grad_out, theta, (((1,), (1,)), ((), ())), preferred_element_type=jnp.float32
    )
    scaled = (grad_z / own_root).astype(jnp.bfloat16)
    gathered = lax.all_gather(scaled, "nets", axis=0, tiled=True)
    theta_term = lax.dot_general(
        saved_agg, grad_out, (((0,), (0,)), ((), ())), preferred_element_type=jnp.float32
    )
    layer_weight_gradient = lax.psum(theta_term, ("cells", "nets")).astype(jnp.bfloat16)
    tile_vals = tile_values[0, 0]
    coords = tile_coords[0, 0]
    live_mask = jnp.arange(tile_vals.shape[0], dtype=jnp.int32) < block_tile_count[0, 0]
    block_cells = gathered.shape[0]
    block_nets = net_pin_count.shape[0]
    tile_len = tile_vals.shape[-1]
    number_of_cells = block_cells // tile_len
    net_count = block_nets // tile_len
    cell_tiles = gathered.reshape(number_of_cells, tile_len, feature_dim)
    net_partial = spread_nets(tile_vals, coords, live_mask, cell_tiles, net_count).reshape(
        block_nets, feature_dim
    )
    net_share = lax.psum_scatter(net_partial, "cells", scatter_dimension=0, tiled=True)
    share_rows = net_share.shape[0]
    share_degree = lax.dynamic_slice_in_dim(net_pin_count, cell_position * share_rows, share_rows)
    gradient_share = (net_share / share_degree.astype(jnp.float32)[:, None]).astype(jnp.bfloat16)
    net_grad = lax.all_gather(gradient_share, "cells", axis=0, tiled=True)
    net_tiles = net_grad.reshape(net_count, tile_len, feature_dim)
    cell_partial = spread_cells(tile_vals, coords, live_mask, net_tiles, number_of_cells).reshape(
        block_cells, feature_dim
    )
    cell_total = lax.psum_scatter(
        cell_partial.astype(jnp.bfloat16), "nets", scatter_dimension=0, tiled=True
    ).astype(jnp.float32)
    grad_cells = (cell_total / own_root).astype(jnp.bfloat16)
    return (grad_cells, layer_weight_gradient)


def exchange_kernel(
    grad_out, saved_agg, theta, tile_values, coords, live, degree, pins,
    out_cells, out_weight,
    go, sa, th, tiles_own, tiles_far, inv_vec, inv_land, inv_own, inv_far, inc, scaled, cells_sum,
    part, part_core, part_x, part_z, part_y, grads,
    wpart, wpart_core, wpart_x, wpart_z, wpart_y, wgrads,
    local_sem, send_sem, recv_sem,
):
    cell = lax.axis_index("cells")
    y = lax.axis_index("nets")
    z, x, core = cell // 4, (cell // 2) % 2, cell % 2

    def device(zt, xt, ct, yt):
        return ((zt * 2 + xt) * 2 + ct, yt)

    to_core = device(z, x, 1 - core, y)
    to_x = device(z, 1 - x, core, y)
    to_y = device(z, x, core, 1 - y)
    z_of = [lax.rem(z + d, 4) for d in range(4)]
    to_z = [device(z_of[d], x, core, y) for d in range(4)]

    loads = [
        pltpu.make_async_copy(src, dst, local_sem.at[i])
        for i, (src, dst) in enumerate(
            ((theta, th), (grad_out, go), (tile_values.at[0, 0], tiles_own.at[pl.ds(0, 16)]), (saved_agg, sa))
        )
    ]
    for load in loads:
        load.start()

    barrier = pltpu.get_barrier_semaphore()
    partners = [to_core, to_x, to_y, to_z[1], to_z[2], to_z[3]]
    for partner in partners:
        pl.semaphore_signal(barrier, inc=1, device_id=partner, device_id_type=MESH)
    pl.semaphore_wait(barrier, len(partners))

    copies = []

    def send(src, dst, target):
        i = len(copies)
        copy = pltpu.make_async_remote_copy(
            src_ref=src, dst_ref=dst, send_sem=send_sem.at[i], recv_sem=recv_sem.at[i],
            device_id=target, device_id_type=MESH,
        )
        copy.start()
        copies.append(copy)
        return copy

    tile_copy = send(tile_values.at[0, 0], tiles_far.at[pl.ds(0, 16)], to_y)
    place = lax.broadcasted_iota(jnp.int32, (8, 128), 1)
    slots = jnp.full((8, 128), 16, jnp.int32)
    for t in range(16):
        code = coords[0, 0, 0, t] * 8 + coords[0, 0, 1, t]
        code = jnp.where(t < live[0, 0], code, -1)
        slots = jnp.where(place == code, t, slots)
    inv_vec[...] = slots
    inv_copy = send(inv_vec, inv_land, to_y)
    own_move = pltpu.make_async_copy(inv_vec, inv_own, local_sem.at[5])
    own_move.start()

    tile_len = tiles_own.shape[-1]
    zero_tile = jnp.zeros((tile_len, tile_len), BF16)
    tiles_own[16] = zero_tile
    tiles_far[16] = zero_tile

    def dense(tiles, inv, block):
        def row(r, carry):
            for j in range(8):
                slot = inv[0, (y * 8 + r) * 8 + j]
                inc[
                    block * 4 + j // 2,
                    pl.ds(pl.multiple_of(r * tile_len, tile_len), tile_len),
                    (j % 2) * tile_len : (j % 2 + 1) * tile_len,
                ] = tiles[slot]
            return carry

        lax.fori_loop(0, 8, row, 0)

    half = scaled.shape[1]
    row_len = part.shape[3]

    def net_part(h, block, xt):
        def pair(p, carry):
            j = block * 4 + xt * 2 + p
            product = jnp.dot(scaled[h], inc[j], preferred_element_type=F32).astype(BF16)
            for q in range(CHUNKS):
                for s in range(2):
                    part[q, h, j * 2 + s] = product[
                        q * row_len : (q + 1) * row_len, s * tile_len : (s + 1) * tile_len
                    ]
            return carry

        lax.fori_loop(0, 2, pair, 0)

    def add(a, b):
        return (a.astype(F32) + b.astype(F32)).astype(BF16)

    def piece(block, xt):
        return pl.ds(block * 8 + xt * 4, 4)

    main = (part, part_core, part_x, part_z, part_y, grads)
    weight = (wpart, wpart_core, wpart_x, wpart_z, wpart_y, wgrads)
    whole, only = pl.ds(0, CHUNKS), pl.ds(0, 1)

    def core_send(st, q, block, xt):
        return send(st[0].at[q, 1 - core, piece(block, xt)], st[1].at[q, piece(block, xt)], to_core)

    def core_add(st, q, copy, block, xt):
        copy.wait_recv()
        at = piece(block, xt)
        st[0][q, core, at] = add(st[0][q, core, at], st[1][q, at])

    def x_send(st, q, block):
        return send(st[0].at[q, core, piece(block, 1 - x)], st[2].at[q, block], to_x)

    def x_add(st, q, copy, block):
        copy.wait_recv()
        at = piece(block, x)
        st[0][q, core, at] = add(st[0][q, core, at], st[2][q, block])

    def tile_of(block, zt):
        return block * 8 + x * 4 + zt

    def z_send(st, q, block):
        return [
            send(st[0].at[q, core, tile_of(block, z_of[d])], st[3].at[q, block, d - 1], to_z[d])
            for d in (1, 2, 3)
        ]

    def z_add(st, q, zs, block):
        total = st[0][q, core, tile_of(block, z)].astype(F32)
        for d in (1, 2, 3):
            zs[d - 1].wait_recv()
            total = total + st[3][q, block, d - 1].astype(F32)
        st[0][q, core, tile_of(block, z)] = total.astype(BF16)

    def y_send(st, q):
        return send(st[0].at[q, core, tile_of(1 - y, z)], st[4].at[q], to_y)

    def y_total(st, q, copy):
        copy.wait_recv()
        return st[0][q, core, tile_of(y, z)].astype(F32) + st[4][q].astype(F32)

    def z_back(st, q):
        at = st[5].at[q, core, tile_of(y, z)]
        return [send(at, at, to_z[d]) for d in (1, 2, 3)]

    def forward(st, q, block, xt, target):
        at = st[5].at[q, core, piece(block, xt)]
        return send(at, at, target)

    loads[0].wait()
    loads[1].wait()
    cells = go.shape[0]
    root = jnp.sqrt(degree[0:1, pl.ds(pl.multiple_of(y * cells, cells), cells)].astype(F32))
    for i in range(4):
        n = cells // 4
        for h in range(2):
            z_rows = lax.dot_general(
                th[h * half : (h + 1) * half], go[i * n : (i + 1) * n], (((1,), (1,)), ((), ())),
                preferred_element_type=F32,
            )
            scaled[h, :, i * n : (i + 1) * n] = (z_rows / root[:, i * n : (i + 1) * n]).astype(BF16)

    loads[2].wait()
    own_move.wait()
    dense(tiles_own, inv_own, y)
    own = {}
    for side in (0, 1):
        xt = 1 - x if side == 0 else x
        net_part(1 - core, y, xt)
        own[side] = core_send(main, whole, y, xt)
        net_part(core, y, xt)
    core_add(main, whole, own[0], y, 1 - x)
    own_x = x_send(main, whole, y)

    loads[3].wait()
    per = wpart.shape[3]

    def weight_rows(i, carry):
        rows = sa[:, pl.ds(pl.multiple_of(i * 128, 128), 128)]
        term = lax.dot_general(rows, go[...], (((0,), (0,)), ((), ())), preferred_element_type=F32)
        term = term.astype(BF16)
        for j in range(128 // per):
            wpart[0, i // 2, (i % 2) * (128 // per) + j] = term[j * per : (j + 1) * per]
        return carry

    lax.fori_loop(0, 4, weight_rows, 0)
    w_core = {}
    for side in (0, 1):
        for block in (0, 1):
            w_core[block, side] = core_send(weight, only, block, 1 - x if side == 0 else x)
    core_add(main, whole, own[1], y, x)
    w_x = []
    for block in (0, 1):
        core_add(weight, only, w_core[block, 0], block, 1 - x)
        w_x.append(x_send(weight, only, block))
    for block in (0, 1):
        core_add(weight, only, w_core[block, 1], block, x)
    x_add(main, whole, own_x, y)
    own_z = z_send(main, whole, y)

    inv_copy.wait_recv()
    inv_move = pltpu.make_async_copy(inv_land, inv_far, local_sem.at[4])
    inv_move.start()
    inv_move.wait()
    tile_copy.wait_recv()
    dense(tiles_far, inv_far, 1 - y)
    far = {}
    chunk = [pl.ds(q, 1) for q in range(CHUNKS)]
    for side in (0, 1):
        xt = 1 - x if side == 0 else x
        net_part(1 - core, 1 - y, xt)
        far[side] = [core_send(main, q, 1 - y, xt) for q in chunk]
        net_part(core, 1 - y, xt)
    w_z = []
    for block in (0, 1):
        x_add(weight, only, w_x[block], block)
        w_z.append(z_send(weight, only, block))

    pin_row = pins[0:1, pl.ds(pl.multiple_of((x * 4 + z) * tile_len, tile_len), tile_len)].astype(F32)
    row_block = 256

    def cell_sum(h, pieces, start=False, last=False):
        def rows(r, carry):
            at = pl.ds(pl.multiple_of(r * row_block, row_block), row_block)
            total = None if start else cells_sum[h, at, :]
            for block, xt in pieces:
                for p in range(2):
                    j = block * 4 + xt * 2 + p
                    net_rows = jnp.concatenate(
                        [
                            jnp.concatenate([grads[q, h, 2 * j], grads[q, h, 2 * j + 1]], axis=1)
                            for q in range(CHUNKS)
                        ],
                        axis=0,
                    )
                    term = lax.dot_general(
                        inc[j, at, :], net_rows, (((1,), (1,)), ((), ())), preferred_element_type=F32
                    )
                    total = term if total is None else total + term
            if not last:
                cells_sum[h, at, :] = total
                return carry
            for i in range(row_block // 128):
                first_row = y * cells + r * row_block + i * 128
                root_row = jnp.sqrt(
                    degree[0:1, pl.ds(pl.multiple_of(first_row, 128), 128)].astype(F32)
                )
                root_tile = jnp.broadcast_to(root_row, (128, 128)).T
                out_at = pl.ds(pl.multiple_of(r * row_block + i * 128, 128), 128)
                for w in range(half // 128):
                    out_cells[out_at, pl.ds(pl.multiple_of(h * half + w * 128, 128), 128)] = (
                        total[i * 128 : (i + 1) * 128, w * 128 : (w + 1) * 128] / root_tile
                    ).astype(BF16)
            return carry

        lax.fori_loop(0, cells // row_block, rows, 0)

    steps = []

    def step(when):
        def put(run):
            steps.append((when, len(steps), run))
            return run

        return put

    def gather_steps(st, q, start, gap, z_copies):
        got = {}

        @step(start)
        def _():
            for copy in z_copies():
                copy.wait_recv()
            got["x"] = forward(st, q, y, x, to_x)
            got["y"] = forward(st, q, y, x, to_y)
            got["core"] = [forward(st, q, y, x, to_core)]

        @step(start + gap)
        def _():
            got["x"].wait_recv()
            got["diagonal"] = forward(st, q, y, 1 - x, to_y)
            got["core"].append(forward(st, q, y, 1 - x, to_core))
            got["y"].wait_recv()
            got["core"].append(forward(st, q, 1 - y, x, to_core))

        @step(start + 2 * gap)
        def _():
            got["diagonal"].wait_recv()
            got["core"].append(forward(st, q, 1 - y, 1 - x, to_core))

        return got

    def chunk_steps(q, start, gap):
        state = {}

        @step(0)
        def _():
            core_add(main, chunk[q], far[0][q], 1 - y, 1 - x)
            state["x"] = x_send(main, chunk[q], 1 - y)

        @step(start + 0.5 * gap)
        def _():
            core_add(main, chunk[q], far[1][q], 1 - y, x)

        @step(start + gap)
        def _():
            x_add(main, chunk[q], state["x"], 1 - y)
            state["z"] = z_send(main, chunk[q], 1 - y)

        @step(start + 2 * gap)
        def _():
            z_add(main, chunk[q], state["z"], 1 - y)
            state["y"] = y_send(main, chunk[q])

        @step(start + 3 * gap)
        def _():
            total = y_total(main, chunk[q], state["y"])
            grads[chunk[q], core, tile_of(y, z)] = (total / pin_row).astype(BF16)
            state["back"] = z_back(main, chunk[q])

        return gather_steps(main, chunk[q], start + 4 * gap, gap, lambda: state["back"])

    gap = 2.0
    got = [chunk_steps(q, q * 1.0, gap) for q in range(CHUNKS)]
    w_state = {}

    @step(0.5 * gap + 0.1)
    def _():
        for block in (0, 1):
            z_add(weight, only, w_z[block], block)
        w_state["y"] = y_send(weight, only)

    @step(1.5 * gap)
    def _():
        z_add(main, whole, own_z, y)

    @step(2 * gap - 0.1)
    def _():
        total = y_total(weight, only, w_state["y"])
        wgrads[only, core, tile_of(y, z)] = total.astype(BF16)
        w_state["back"] = z_back(weight, only)

    w_got = gather_steps(weight, only, 3 * gap + 0.1, 1.5 * gap, lambda: w_state["back"])
    late = 4 * gap + CHUNKS - 1

    @step(late + 0.1)
    def _():
        cell_sum(core, [(y, x)], start=True)

    @step(late + gap + 0.1)
    def _():
        for q in range(CHUNKS):
            got[q]["core"][0].wait_recv()
        cell_sum(1 - core, [(y, x)], start=True)
        cell_sum(core, [(1 - y, x), (y, 1 - x)])

    for _, _, run in sorted(steps, key=lambda entry: entry[:2]):
        run()

    for q in range(CHUNKS):
        got[q]["core"][1].wait_recv()
        got[q]["core"][2].wait_recv()
    cell_sum(1 - core, [(1 - y, x), (y, 1 - x)])
    cell_sum(core, [(1 - y, 1 - x)], last=True)
    for copy in w_got["core"]:
        copy.wait_recv()
    for t in range(32):
        out_weight[t * per : (t + 1) * per, :] = wgrads[0, t // 16, t % 16]
    for q in range(CHUNKS):
        got[q]["core"][3].wait_recv()
    cell_sum(1 - core, [(1 - y, 1 - x)], last=True)
    for copy in copies:
        copy.wait_send()


def fused_shards(
    grad_out, saved_agg, theta, tile_values, tile_coords, block_tile_count, cell_degree, net_pin_count
):
    rows, width = grad_out.shape
    slots, tile_len = tile_values.shape[2], tile_values.shape[3]
    nets = net_pin_count.shape[0]
    net_tiles = nets // tile_len
    half, row_len = width // 2, width // 2 // CHUNKS
    per = width // 32
    vmem = pltpu.VMEM
    any_spec = pl.BlockSpec(memory_space=pl.ANY)
    vmem_spec = pl.BlockSpec(memory_space=pltpu.VMEM)

    def stage_buffers(lead, block):
        return [
            vmem(lead + (2, 16) + block, BF16),
            vmem(lead + (16,) + block, BF16),
            vmem(lead + (2, 4) + block, BF16),
            vmem(lead + (2, 3) + block, BF16),
            vmem(lead + block, BF16),
            vmem(lead + (2, 16) + block, BF16),
        ]

    return pl.pallas_call(
        exchange_kernel,
        out_shape=(
            jax.ShapeDtypeStruct((rows, width), BF16),
            jax.ShapeDtypeStruct((width, width), BF16),
        ),
        in_specs=[any_spec] * 4
        + [pl.BlockSpec(memory_space=pltpu.SMEM)] * 2 + [vmem_spec] * 2,
        out_specs=(vmem_spec, vmem_spec),
        scratch_shapes=[
            vmem((rows, width), BF16),
            vmem((rows, width), BF16),
            vmem((width, width), BF16),
            vmem((slots + 1, tile_len, tile_len), BF16),
            vmem((slots + 1, tile_len, tile_len), BF16),
            vmem((8, 128), jnp.int32),
            vmem((8, 128), jnp.int32),
            pltpu.SMEM((8, 128), jnp.int32),
            pltpu.SMEM((8, 128), jnp.int32),
            vmem((net_tiles, rows, 2 * tile_len), BF16),
            vmem((2, half, rows), BF16),
            vmem((2, rows, half), F32),
        ]
        + stage_buffers((CHUNKS,), (row_len, tile_len))
        + stage_buffers((1,), (per, width))
        + [
            pltpu.SemaphoreType.DMA((8,)),
            pltpu.SemaphoreType.DMA((160,)),
            pltpu.SemaphoreType.DMA((160,)),
        ],
        compiler_params=pltpu.CompilerParams(
            collective_id=0, has_side_effects=True, vmem_limit_bytes=60 * 1024 * 1024
        ),
    )(
        grad_out, saved_agg, theta, tile_values, jnp.swapaxes(tile_coords, 2, 3), block_tile_count,
        cell_degree.reshape(1, -1), net_pin_count.reshape(1, -1),
    )


def solution(mesh):
    in_specs = (
        P(("cells", "nets"), None),
        P(("cells", "nets"), None),
        P(),
        P("cells", "nets", None, None, None),
        P("cells", "nets", None, None),
        P("cells", "nets"),
        P("cells"),
        P("nets"),
    )
    fused = mesh.shape["cells"] == 16 and mesh.shape["nets"] == 2
    out_specs = (P(("cells", "nets"), None), P())
    return jax.shard_map(
        fused_shards if fused else shards, mesh=mesh, in_specs=in_specs, out_specs=out_specs, check_vma=False,
    )
```

```python
import functools

import jax
import jax.numpy as jnp
from jax import lax
from jax.experimental import pallas as pl
from jax.experimental.pallas import tpu as pltpu
from jax.sharding import PartitionSpec as P

TBLK = 16
CHUNKS = 4
F32 = jnp.float32
BF16 = jnp.bfloat16
MESH = pl.DeviceIdType.MESH


def spread_nets(tile_vals, coords, live_mask, cell_tiles, net_count):
    tile_len = tile_vals.shape[-1]
    feature_dim = cell_tiles.shape[-1]
    running = jnp.zeros((net_count, tile_len, feature_dim), jnp.float32)
    selected_tiles = cell_tiles[coords[0:TBLK, 0]]
    matrix_product = jnp.einsum(
        "cnr,cnw->crw", tile_vals, selected_tiles, preferred_element_type=jnp.float32
    )
    weight = live_mask.astype(jnp.float32)[:, None, None]
    running = running.at[coords[0:TBLK, 1]].add(matrix_product * weight)
    return running


def spread_cells(tile_vals, coords, live_mask, net_tiles, number_of_cells):
    tile_len = tile_vals.shape[-1]
    feature_dim = net_tiles.shape[-1]
    running = jnp.zeros((number_of_cells, tile_len, feature_dim), jnp.float32)
    selected_tiles = net_tiles[coords[0:TBLK, 1]]
    matrix_product = jnp.einsum(
        "jaf,jfw->jaw", tile_vals, selected_tiles, preferred_element_type=jnp.float32
    )
    weight = live_mask.astype(jnp.float32)[:, None, None]
    running = running.at[coords[0:TBLK, 0]].add(matrix_product * weight)
    return running


def shards(
    grad_out,
    saved_agg,
    theta,
    tile_values,
    tile_coords,
    block_tile_count,
    cell_degree,
    net_pin_count,
):
    own_rows = grad_out.shape[0]
    feature_dim = grad_out.shape[1]
    net_position = lax.axis_index("nets")
    cell_position = lax.axis_index("cells")
    own_degree = lax.dynamic_slice_in_dim(cell_degree, net_position * own_rows, own_rows)
    own_root = jnp.sqrt(own_degree.astype(jnp.float32))[:, None]
    grad_z = lax.dot_general(
        grad_out, theta, (((1,), (1,)), ((), ())), preferred_element_type=jnp.float32
    )
    scaled = (grad_z / own_root).astype(jnp.bfloat16)
    gathered = lax.all_gather(scaled, "nets", axis=0, tiled=True)
    theta_term = lax.dot_general(
        saved_agg, grad_out, (((0,), (0,)), ((), ())), preferred_element_type=jnp.float32
    )
    layer_weight_gradient = lax.psum(theta_term, ("cells", "nets")).astype(jnp.bfloat16)
    tile_vals = tile_values[0, 0]
    coords = tile_coords[0, 0]
    live_mask = jnp.arange(tile_vals.shape[0], dtype=jnp.int32) < block_tile_count[0, 0]
    block_cells = gathered.shape[0]
    block_nets = net_pin_count.shape[0]
    tile_len = tile_vals.shape[-1]
    number_of_cells = block_cells // tile_len
    net_count = block_nets // tile_len
    cell_tiles = gathered.reshape(number_of_cells, tile_len, feature_dim)
    net_partial = spread_nets(tile_vals, coords, live_mask, cell_tiles, net_count).reshape(
        block_nets, feature_dim
    )
    net_share = lax.psum_scatter(net_partial, "cells", scatter_dimension=0, tiled=True)
    share_rows = net_share.shape[0]
    share_degree = lax.dynamic_slice_in_dim(net_pin_count, cell_position * share_rows, share_rows)
    gradient_share = (net_share / share_degree.astype(jnp.float32)[:, None]).astype(jnp.bfloat16)
    net_grad = lax.all_gather(gradient_share, "cells", axis=0, tiled=True)
    net_tiles = net_grad.reshape(net_count, tile_len, feature_dim)
    cell_partial = spread_cells(tile_vals, coords, live_mask, net_tiles, number_of_cells).reshape(
        block_cells, feature_dim
    )
    cell_total = lax.psum_scatter(
        cell_partial.astype(jnp.bfloat16), "nets", scatter_dimension=0, tiled=True
    ).astype(jnp.float32)
    grad_cells = (cell_total / own_root).astype(jnp.bfloat16)
    return (grad_cells, layer_weight_gradient)


def exchange_kernel(
    grad_out, saved_agg, theta, tile_values, coords, live, degree, pins,
    out_cells, out_weight,
    go, sa, th, tiles_own, tiles_far, inv_vec, inv_land, inv_own, inv_far, inc, scaled, cells_sum,
    part, part_core, part_x, part_z, part_y, grads,
    wpart, wpart_core, wpart_x, wpart_z, wpart_y, wgrads,
    local_sem, send_sem, recv_sem, pair_send, pair_recv,
):
    cell = lax.axis_index("cells")
    y = lax.axis_index("nets")
    z, x, core = cell // 4, (cell // 2) % 2, cell % 2

    def device(zt, xt, ct, yt):
        return ((zt * 2 + xt) * 2 + ct, yt)

    to_core = device(z, x, 1 - core, y)
    to_x = device(z, 1 - x, core, y)
    to_y = device(z, x, core, 1 - y)
    z_of = [lax.rem(z + d, 4) for d in range(4)]
    to_z = [device(z_of[d], x, core, y) for d in range(4)]

    loads = [
        pltpu.make_async_copy(src, dst, local_sem.at[i])
        for i, (src, dst) in enumerate(
            ((theta, th), (grad_out, go), (tile_values.at[0, 0], tiles_own.at[pl.ds(0, 16)]), (saved_agg, sa))
        )
    ]
    for load in loads:
        load.start()

    barrier = pltpu.get_barrier_semaphore()
    partners = [to_core, to_x, to_y, to_z[1], to_z[2], to_z[3]]
    for partner in partners:
        pl.semaphore_signal(barrier, inc=1, device_id=partner, device_id_type=MESH)
    pl.semaphore_wait(barrier, len(partners))

    copies = []

    def send(src, dst, target):
        i = len(copies)
        copy = pltpu.make_async_remote_copy(
            src_ref=src, dst_ref=dst, send_sem=send_sem.at[i], recv_sem=recv_sem.at[i],
            device_id=target, device_id_type=MESH,
        )
        copy.start()
        copies.append(copy)
        return copy

    tile_copy = send(tile_values.at[0, 0], tiles_far.at[pl.ds(0, 16)], to_y)
    place = lax.broadcasted_iota(jnp.int32, (8, 128), 1)
    slots = jnp.full((8, 128), 16, jnp.int32)
    for t in range(16):
        code = coords[0, 0, 0, t] * 8 + coords[0, 0, 1, t]
        code = jnp.where(t < live[0, 0], code, -1)
        slots = jnp.where(place == code, t, slots)
    inv_vec[...] = slots
    inv_copy = send(inv_vec, inv_land, to_y)
    own_move = pltpu.make_async_copy(inv_vec, inv_own, local_sem.at[5])
    own_move.start()

    tile_len = tiles_own.shape[-1]
    zero_tile = jnp.zeros((tile_len, tile_len), BF16)
    tiles_own[16] = zero_tile
    tiles_far[16] = zero_tile

    def dense(tiles, inv, block):
        def row(r, carry):
            for j in range(8):
                slot = inv[0, (y * 8 + r) * 8 + j]
                inc[
                    block * 4 + j // 2,
                    pl.ds(pl.multiple_of(r * tile_len, tile_len), tile_len),
                    (j % 2) * tile_len : (j % 2 + 1) * tile_len,
                ] = tiles[slot]
            return carry

        lax.fori_loop(0, 8, row, 0)

    half = scaled.shape[0] // 2
    row_len = part.shape[3]

    def core_copy(block, p):
        pair = block * 4 + lax.rem((1 - x) * 2 + p, 4)
        i = (block + y) % 2 * 4 + p
        at = pl.ds(pair * 2, 2)
        return pltpu.make_async_remote_copy(
            src_ref=part.at[:, 1 - core, at], dst_ref=part_core.at[:, at],
            send_sem=pair_send.at[i], recv_sem=pair_recv.at[i],
            device_id=to_core, device_id_type=MESH,
        )

    def net_part(block):
        def step(p, carry):
            j = block * 4 + lax.rem((1 - x) * 2 + p, 4)
            product = jnp.dot(scaled[...], inc[j], preferred_element_type=F32).astype(BF16)
            for h in range(2):
                for q in range(CHUNKS):
                    row = h * half + q * row_len
                    for s in range(2):
                        part[q, h, j * 2 + s] = product[
                            row : row + row_len, s * tile_len : (s + 1) * tile_len
                        ]
            core_copy(block, p).start()
            return carry

        lax.fori_loop(0, 4, step, 0)

    def add(a, b):
        return (a.astype(F32) + b.astype(F32)).astype(BF16)

    def piece(block, xt):
        return pl.ds(block * 8 + xt * 4, 4)

    main = (part, part_core, part_x, part_z, part_y, grads)
    weight = (wpart, wpart_core, wpart_x, wpart_z, wpart_y, wgrads)
    whole, only = pl.ds(0, CHUNKS), pl.ds(0, 1)

    def core_send(st, q, block, xt):
        return send(st[0].at[q, 1 - core, piece(block, xt)], st[1].at[q, piece(block, xt)], to_core)

    def core_add(st, q, copy, block, xt):
        if copy is not None:
            copy.wait_recv()
        at = piece(block, xt)
        st[0][q, core, at] = add(st[0][q, core, at], st[1][q, at])

    def x_send(st, q, block):
        return send(st[0].at[q, core, piece(block, 1 - x)], st[2].at[q, block], to_x)

    def x_add(st, q, copy, block):
        copy.wait_recv()
        at = piece(block, x)
        st[0][q, core, at] = add(st[0][q, core, at], st[2][q, block])

    def tile_of(block, zt):
        return block * 8 + x * 4 + zt

    def z_send(st, q, block):
        return [
            send(st[0].at[q, core, tile_of(block, z_of[d])], st[3].at[q, block, d - 1], to_z[d])
            for d in (1, 2, 3)
        ]

    def z_add(st, q, zs, block):
        total = st[0][q, core, tile_of(block, z)].astype(F32)
        for d in (1, 2, 3):
            zs[d - 1].wait_recv()
            total = total + st[3][q, block, d - 1].astype(F32)
        st[0][q, core, tile_of(block, z)] = total.astype(BF16)

    def y_send(st, q):
        return send(st[0].at[q, core, tile_of(1 - y, z)], st[4].at[q], to_y)

    def y_total(st, q, copy):
        copy.wait_recv()
        return st[0][q, core, tile_of(y, z)].astype(F32) + st[4][q].astype(F32)

    def z_back(st, q):
        at = st[5].at[q, core, tile_of(y, z)]
        return [send(at, at, to_z[d]) for d in (1, 2, 3)]

    def forward(st, q, block, xt, target):
        at = st[5].at[q, core, piece(block, xt)]
        return send(at, at, target)

    loads[0].wait()
    loads[1].wait()
    cells = go.shape[0]

    def scale_rows(i, carry):
        at = pl.ds(pl.multiple_of(i * 256, 256), 256)
        z_rows = lax.dot_general(
            th[...], go[at, :], (((1,), (1,)), ((), ())), preferred_element_type=F32
        )
        at_degree = pl.ds(pl.multiple_of(y * cells + i * 256, 256), 256)
        root = jnp.sqrt(degree[0:1, at_degree].astype(F32))
        scaled[:, at] = (z_rows / root).astype(BF16)
        return carry

    lax.fori_loop(0, cells // 256, scale_rows, 0)
    loads[2].wait()
    own_move.wait()
    dense(tiles_own, inv_own, y)
    net_part(y)
    for p in (0, 1):
        core_copy(y, p).wait_recv()
    core_add(main, whole, None, y, 1 - x)
    own_x = x_send(main, whole, y)

    loads[3].wait()
    per = wpart.shape[3]

    def weight_rows(i, carry):
        rows = sa[:, pl.ds(pl.multiple_of(i * 128, 128), 128)]
        term = lax.dot_general(rows, go[...], (((0,), (0,)), ((), ())), preferred_element_type=F32)
        term = term.astype(BF16)
        for j in range(128 // per):
            wpart[0, i // 2, (i % 2) * (128 // per) + j] = term[j * per : (j + 1) * per]
        return carry

    lax.fori_loop(0, 4, weight_rows, 0)
    w_core = {}
    for side in (0, 1):
        for block in (0, 1):
            w_core[block, side] = core_send(weight, only, block, 1 - x if side == 0 else x)
    for p in (2, 3):
        core_copy(y, p).wait_recv()
    core_add(main, whole, None, y, x)
    w_x = []
    for block in (0, 1):
        core_add(weight, only, w_core[block, 0], block, 1 - x)
        w_x.append(x_send(weight, only, block))
    for block in (0, 1):
        core_add(weight, only, w_core[block, 1], block, x)
    x_add(main, whole, own_x, y)
    own_z = z_send(main, whole, y)

    inv_copy.wait_recv()
    inv_move = pltpu.make_async_copy(inv_land, inv_far, local_sem.at[4])
    inv_move.start()
    inv_move.wait()
    tile_copy.wait_recv()
    dense(tiles_far, inv_far, 1 - y)
    chunk = [pl.ds(q, 1) for q in range(CHUNKS)]
    net_part(1 - y)
    w_z = []
    for block in (0, 1):
        x_add(weight, only, w_x[block], block)
        w_z.append(z_send(weight, only, block))

    pin_row = pins[0:1, pl.ds(pl.multiple_of((x * 4 + z) * tile_len, tile_len), tile_len)].astype(F32)
    row_block = 256

    def cell_sum(h, pieces, start=False):
        def rows(r, carry):
            at = pl.ds(pl.multiple_of(lax.rem(r, 4) * row_block, row_block), row_block)
            block, xt = pieces(r // 4)
            total = None if start else cells_sum[h, at, :]
            for p in range(2):
                j = block * 4 + xt * 2 + p
                net_rows = jnp.concatenate(
                    [
                        jnp.concatenate([grads[q, h, 2 * j], grads[q, h, 2 * j + 1]], axis=1)
                        for q in range(CHUNKS)
                    ],
                    axis=0,
                )
                term = lax.dot_general(
                    inc[j, at, :], net_rows, (((1,), (1,)), ((), ())), preferred_element_type=F32
                )
                total = term if total is None else total + term
            cells_sum[h, at, :] = total
            return carry

        return rows

    def run_sum(h, pieces, count, start=False):
        lax.fori_loop(0, count * (cells // row_block), cell_sum(h, pieces, start), 0)

    def sides(i):
        return lax.rem(1 - y + i, 2), lax.rem(x + i, 2)

    def store_rows(i, carry):
        at = pl.ds(pl.multiple_of(i * 128, 128), 128)
        at_degree = pl.ds(pl.multiple_of(y * cells + i * 128, 128), 128)
        root_row = jnp.sqrt(degree[0:1, at_degree].astype(F32))
        root_tile = jnp.broadcast_to(root_row, (128, 128)).T
        for h in range(2):
            for w in range(half // 128):
                out_cells[at, h * half + w * 128 : h * half + (w + 1) * 128] = (
                    cells_sum[h, at, w * 128 : (w + 1) * 128] / root_tile
                ).astype(BF16)
        return carry

    steps = []

    def step(when):
        def put(run):
            steps.append((when, len(steps), run))
            return run

        return put

    def gather_steps(st, q, start, gap, z_copies):
        got = {}

        @step(start)
        def _():
            for copy in z_copies():
                copy.wait_recv()
            got["x"] = forward(st, q, y, x, to_x)
            got["y"] = forward(st, q, y, x, to_y)
            got["core"] = [forward(st, q, y, x, to_core)]

        @step(start + gap)
        def _():
            got["x"].wait_recv()
            got["diagonal"] = forward(st, q, y, 1 - x, to_y)
            got["core"].append(forward(st, q, y, 1 - x, to_core))
            got["y"].wait_recv()
            got["core"].append(forward(st, q, 1 - y, x, to_core))

        @step(start + 2 * gap)
        def _():
            got["diagonal"].wait_recv()
            got["core"].append(forward(st, q, 1 - y, 1 - x, to_core))

        return got

    def chunk_steps(q, start, gap):
        state = {}

        @step(0)
        def _():
            if q == 0:
                for p in (0, 1):
                    core_copy(1 - y, p).wait_recv()
            core_add(main, chunk[q], None, 1 - y, 1 - x)
            state["x"] = x_send(main, chunk[q], 1 - y)

        @step(start + 0.5 * gap)
        def _():
            if q == 0:
                for p in (2, 3):
                    core_copy(1 - y, p).wait_recv()
            core_add(main, chunk[q], None, 1 - y, x)

        @step(start + gap)
        def _():
            x_add(main, chunk[q], state["x"], 1 - y)
            state["z"] = z_send(main, chunk[q], 1 - y)

        @step(start + 2 * gap)
        def _():
            z_add(main, chunk[q], state["z"], 1 - y)
            state["y"] = y_send(main, chunk[q])

        @step(start + 3 * gap)
        def _():
            total = y_total(main, chunk[q], state["y"])
            grads[chunk[q], core, tile_of(y, z)] = (total / pin_row).astype(BF16)
            state["back"] = z_back(main, chunk[q])

        return gather_steps(main, chunk[q], start + 4 * gap, gap, lambda: state["back"])

    gap = 2.0
    got = [chunk_steps(q, q * 1.0, gap) for q in range(CHUNKS)]
    w_state = {}

    @step(0.5 * gap + 0.1)
    def _():
        for block in (0, 1):
            z_add(weight, only, w_z[block], block)
        w_state["y"] = y_send(weight, only)

    @step(1.5 * gap)
    def _():
        z_add(main, whole, own_z, y)

    @step(2 * gap - 0.1)
    def _():
        total = y_total(weight, only, w_state["y"])
        wgrads[only, core, tile_of(y, z)] = total.astype(BF16)
        w_state["back"] = z_back(weight, only)

    w_got = gather_steps(weight, only, 3 * gap + 0.1, 1.5 * gap, lambda: w_state["back"])
    late = 4 * gap + CHUNKS - 1

    @step(late + 0.1)
    def _():
        run_sum(core, lambda i: (y, x), 1, start=True)

    @step(late + gap + 0.1)
    def _():
        for q in range(CHUNKS):
            got[q]["core"][0].wait_recv()
        run_sum(1 - core, lambda i: (y, x), 1, start=True)
        run_sum(core, sides, 2)

    for _, _, run in sorted(steps, key=lambda entry: entry[:2]):
        run()

    for q in range(CHUNKS):
        got[q]["core"][1].wait_recv()
        got[q]["core"][2].wait_recv()
    run_sum(1 - core, sides, 2)
    run_sum(core, lambda i: (1 - y, 1 - x), 1)
    for copy in w_got["core"]:
        copy.wait_recv()

    def store_weight(t, carry):
        out_weight[pl.ds(pl.multiple_of(t * per, per), per), :] = wgrads[0, t // 16, lax.rem(t, 16)]
        return carry

    lax.fori_loop(0, 32, store_weight, 0)
    for q in range(CHUNKS):
        got[q]["core"][3].wait_recv()
    run_sum(1 - core, lambda i: (1 - y, 1 - x), 1)
    lax.fori_loop(0, cells // 128, store_rows, 0)
    for block in (y, 1 - y):
        for p in range(4):
            core_copy(block, p).wait_send()
    for copy in copies:
        copy.wait_send()


def fused_shards(
    grad_out, saved_agg, theta, tile_values, tile_coords, block_tile_count, cell_degree, net_pin_count
):
    rows, width = grad_out.shape
    slots, tile_len = tile_values.shape[2], tile_values.shape[3]
    nets = net_pin_count.shape[0]
    net_tiles = nets // tile_len
    half, row_len = width // 2, width // 2 // CHUNKS
    per = width // 32
    vmem = pltpu.VMEM
    any_spec = pl.BlockSpec(memory_space=pl.ANY)
    vmem_spec = pl.BlockSpec(memory_space=pltpu.VMEM)

    def stage_buffers(lead, block):
        return [
            vmem(lead + (2, 16) + block, BF16),
            vmem(lead + (16,) + block, BF16),
            vmem(lead + (2, 4) + block, BF16),
            vmem(lead + (2, 3) + block, BF16),
            vmem(lead + block, BF16),
            vmem(lead + (2, 16) + block, BF16),
        ]

    return pl.pallas_call(
        exchange_kernel,
        out_shape=(
            pltpu.VMEM((rows, width), BF16),
            pltpu.VMEM((width, width), BF16),
        ),
        in_specs=[any_spec] * 4
        + [pl.BlockSpec(memory_space=pltpu.SMEM)] * 2 + [vmem_spec] * 2,
        out_specs=(vmem_spec, vmem_spec),
        scratch_shapes=[
            vmem((rows, width), BF16),
            vmem((rows, width), BF16),
            vmem((width, width), BF16),
            vmem((slots + 1, tile_len, tile_len), BF16),
            vmem((slots + 1, tile_len, tile_len), BF16),
            vmem((8, 128), jnp.int32),
            vmem((8, 128), jnp.int32),
            pltpu.SMEM((8, 128), jnp.int32),
            pltpu.SMEM((8, 128), jnp.int32),
            vmem((net_tiles, rows, 2 * tile_len), BF16),
            vmem((width, rows), BF16),
            vmem((2, rows, half), F32),
        ]
        + stage_buffers((CHUNKS,), (row_len, tile_len))
        + stage_buffers((1,), (per, width))
        + [
            pltpu.SemaphoreType.DMA((8,)),
            pltpu.SemaphoreType.DMA((160,)),
            pltpu.SemaphoreType.DMA((160,)),
            pltpu.SemaphoreType.DMA((8,)),
            pltpu.SemaphoreType.DMA((8,)),
        ],
        compiler_params=pltpu.CompilerParams(
            collective_id=0, has_side_effects=True, vmem_limit_bytes=60 * 1024 * 1024
        ),
    )(
        grad_out, saved_agg, theta, tile_values, jnp.swapaxes(tile_coords, 2, 3), block_tile_count,
        cell_degree.reshape(1, -1), net_pin_count.reshape(1, -1),
    )


def solution(mesh):
    in_specs = (
        P(("cells", "nets"), None),
        P(("cells", "nets"), None),
        P(),
        P("cells", "nets", None, None, None),
        P("cells", "nets", None, None),
        P("cells", "nets"),
        P("cells"),
        P("nets"),
    )
    fused = mesh.shape["cells"] == 16 and mesh.shape["nets"] == 2
    out_specs = (P(("cells", "nets"), None), P())
    return jax.shard_map(
        fused_shards if fused else shards, mesh=mesh, in_specs=in_specs, out_specs=out_specs, check_vma=False,
    )
```

```python
import functools

import jax
import jax.numpy as jnp
from jax import lax
from jax.experimental import pallas as pl
from jax.experimental.pallas import tpu as pltpu
from jax.sharding import PartitionSpec as P

TBLK = 16
CHUNKS = 2
F32 = jnp.float32
BF16 = jnp.bfloat16
MESH = pl.DeviceIdType.MESH


def spread_nets(tile_vals, coords, live_mask, cell_tiles, net_count):
    tile_len = tile_vals.shape[-1]
    feature_dim = cell_tiles.shape[-1]
    running = jnp.zeros((net_count, tile_len, feature_dim), jnp.float32)
    selected_tiles = cell_tiles[coords[0:TBLK, 0]]
    matrix_product = jnp.einsum(
        "cnr,cnw->crw", tile_vals, selected_tiles, preferred_element_type=jnp.float32
    )
    weight = live_mask.astype(jnp.float32)[:, None, None]
    running = running.at[coords[0:TBLK, 1]].add(matrix_product * weight)
    return running


def spread_cells(tile_vals, coords, live_mask, net_tiles, number_of_cells):
    tile_len = tile_vals.shape[-1]
    feature_dim = net_tiles.shape[-1]
    running = jnp.zeros((number_of_cells, tile_len, feature_dim), jnp.float32)
    selected_tiles = net_tiles[coords[0:TBLK, 1]]
    matrix_product = jnp.einsum(
        "jaf,jfw->jaw", tile_vals, selected_tiles, preferred_element_type=jnp.float32
    )
    weight = live_mask.astype(jnp.float32)[:, None, None]
    running = running.at[coords[0:TBLK, 0]].add(matrix_product * weight)
    return running


def shards(
    grad_out,
    saved_agg,
    theta,
    tile_values,
    tile_coords,
    block_tile_count,
    cell_degree,
    net_pin_count,
):
    own_rows = grad_out.shape[0]
    feature_dim = grad_out.shape[1]
    net_position = lax.axis_index("nets")
    cell_position = lax.axis_index("cells")
    own_degree = lax.dynamic_slice_in_dim(cell_degree, net_position * own_rows, own_rows)
    own_root = jnp.sqrt(own_degree.astype(jnp.float32))[:, None]
    grad_z = lax.dot_general(
        grad_out, theta, (((1,), (1,)), ((), ())), preferred_element_type=jnp.float32
    )
    scaled = (grad_z / own_root).astype(jnp.bfloat16)
    gathered = lax.all_gather(scaled, "nets", axis=0, tiled=True)
    theta_term = lax.dot_general(
        saved_agg, grad_out, (((0,), (0,)), ((), ())), preferred_element_type=jnp.float32
    )
    layer_weight_gradient = lax.psum(theta_term, ("cells", "nets")).astype(jnp.bfloat16)
    tile_vals = tile_values[0, 0]
    coords = tile_coords[0, 0]
    live_mask = jnp.arange(tile_vals.shape[0], dtype=jnp.int32) < block_tile_count[0, 0]
    block_cells = gathered.shape[0]
    block_nets = net_pin_count.shape[0]
    tile_len = tile_vals.shape[-1]
    number_of_cells = block_cells // tile_len
    net_count = block_nets // tile_len
    cell_tiles = gathered.reshape(number_of_cells, tile_len, feature_dim)
    net_partial = spread_nets(tile_vals, coords, live_mask, cell_tiles, net_count).reshape(
        block_nets, feature_dim
    )
    net_share = lax.psum_scatter(net_partial, "cells", scatter_dimension=0, tiled=True)
    share_rows = net_share.shape[0]
    share_degree = lax.dynamic_slice_in_dim(net_pin_count, cell_position * share_rows, share_rows)
    gradient_share = (net_share / share_degree.astype(jnp.float32)[:, None]).astype(jnp.bfloat16)
    net_grad = lax.all_gather(gradient_share, "cells", axis=0, tiled=True)
    net_tiles = net_grad.reshape(net_count, tile_len, feature_dim)
    cell_partial = spread_cells(tile_vals, coords, live_mask, net_tiles, number_of_cells).reshape(
        block_cells, feature_dim
    )
    cell_total = lax.psum_scatter(
        cell_partial.astype(jnp.bfloat16), "nets", scatter_dimension=0, tiled=True
    ).astype(jnp.float32)
    grad_cells = (cell_total / own_root).astype(jnp.bfloat16)
    return (grad_cells, layer_weight_gradient)


def exchange_kernel(
    grad_out, saved_agg, theta, tile_values, coords, live, degree, pins,
    out_cells, out_weight,
    go, sa, th, tiles_own, tiles_far, inv_vec, inv_land, inv_own, inv_far, inc, scaled, cells_sum,
    part, part_core, part_x, part_z, part_y, grads,
    wpart, wpart_core, wpart_x, wpart_z, wpart_y, wgrads,
    local_sem, send_sem, recv_sem,
):
    cell = lax.axis_index("cells")
    y = lax.axis_index("nets")
    z, x, core = cell // 4, (cell // 2) % 2, cell % 2

    def device(zt, xt, ct, yt):
        return ((zt * 2 + xt) * 2 + ct, yt)

    to_core = device(z, x, 1 - core, y)
    to_x = device(z, 1 - x, core, y)
    to_y = device(z, x, core, 1 - y)
    z_of = [lax.rem(z + d, 4) for d in range(4)]
    to_z = [device(z_of[d], x, core, y) for d in range(4)]

    loads = [
        pltpu.make_async_copy(src, dst, local_sem.at[i])
        for i, (src, dst) in enumerate(
            ((theta, th), (grad_out, go), (tile_values.at[0, 0], tiles_own.at[pl.ds(0, 16)]), (saved_agg, sa))
        )
    ]
    for load in loads:
        load.start()

    barrier = pltpu.get_barrier_semaphore()
    partners = [to_core, to_x, to_y, to_z[1], to_z[2], to_z[3]]
    for partner in partners:
        pl.semaphore_signal(barrier, inc=1, device_id=partner, device_id_type=MESH)
    pl.semaphore_wait(barrier, len(partners))

    copies = []

    def send(src, dst, target):
        i = len(copies)
        copy = pltpu.make_async_remote_copy(
            src_ref=src, dst_ref=dst, send_sem=send_sem.at[i], recv_sem=recv_sem.at[i],
            device_id=target, device_id_type=MESH,
        )
        copy.start()
        copies.append(copy)
        return copy

    tile_copy = send(tile_values.at[0, 0], tiles_far.at[pl.ds(0, 16)], to_y)
    place = lax.broadcasted_iota(jnp.int32, (8, 128), 1)
    slots = jnp.full((8, 128), 16, jnp.int32)
    for t in range(16):
        code = coords[0, 0, 0, t] * 8 + coords[0, 0, 1, t]
        code = jnp.where(t < live[0, 0], code, -1)
        slots = jnp.where(place == code, t, slots)
    inv_vec[...] = slots
    inv_copy = send(inv_vec, inv_land, to_y)
    own_move = pltpu.make_async_copy(inv_vec, inv_own, local_sem.at[5])
    own_move.start()

    tile_len = tiles_own.shape[-1]
    zero_tile = jnp.zeros((tile_len, tile_len), BF16)
    tiles_own[16] = zero_tile
    tiles_far[16] = zero_tile

    def dense(tiles, inv, block):
        def row(r, carry):
            for j in range(8):
                slot = inv[0, (y * 8 + r) * 8 + j]
                inc[
                    block * 4 + j // 2,
                    pl.ds(pl.multiple_of(r * tile_len, tile_len), tile_len),
                    (j % 2) * tile_len : (j % 2 + 1) * tile_len,
                ] = tiles[slot]
            return carry

        lax.fori_loop(0, 8, row, 0)

    half = scaled.shape[1]
    row_len = part.shape[3]

    def net_part(h, block, xt):
        def pair(p, carry):
            j = block * 4 + xt * 2 + p
            product = jnp.dot(scaled[h], inc[j], preferred_element_type=F32).astype(BF16)
            for q in range(CHUNKS):
                for s in range(2):
                    part[q, h, j * 2 + s] = product[
                        q * row_len : (q + 1) * row_len, s * tile_len : (s + 1) * tile_len
                    ]
            return carry

        lax.fori_loop(0, 2, pair, 0)

    def add(a, b):
        return (a.astype(F32) + b.astype(F32)).astype(BF16)

    def piece(block, xt):
        return pl.ds(block * 8 + xt * 4, 4)

    main = (part, part_core, part_x, part_z, part_y, grads)
    weight = (wpart, wpart_core, wpart_x, wpart_z, wpart_y, wgrads)
    whole, only = pl.ds(0, CHUNKS), pl.ds(0, 1)

    def core_send(st, q, block, xt):
        return send(st[0].at[q, 1 - core, piece(block, xt)], st[1].at[q, piece(block, xt)], to_core)

    def core_add(st, q, copy, block, xt):
        copy.wait_recv()
        at = piece(block, xt)
        st[0][q, core, at] = add(st[0][q, core, at], st[1][q, at])

    def x_send(st, q, block):
        return send(st[0].at[q, core, piece(block, 1 - x)], st[2].at[q, block], to_x)

    def x_add(st, q, copy, block):
        copy.wait_recv()
        at = piece(block, x)
        st[0][q, core, at] = add(st[0][q, core, at], st[2][q, block])

    def tile_of(block, zt):
        return block * 8 + x * 4 + zt

    def z_send(st, q, block):
        return [
            send(st[0].at[q, core, tile_of(block, z_of[d])], st[3].at[q, block, d - 1], to_z[d])
            for d in (1, 2, 3)
        ]

    def z_add(st, q, zs, block):
        total = st[0][q, core, tile_of(block, z)].astype(F32)
        for d in (1, 2, 3):
            zs[d - 1].wait_recv()
            total = total + st[3][q, block, d - 1].astype(F32)
        st[0][q, core, tile_of(block, z)] = total.astype(BF16)

    def y_send(st, q):
        return send(st[0].at[q, core, tile_of(1 - y, z)], st[4].at[q], to_y)

    def y_total(st, q, copy):
        copy.wait_recv()
        return st[0][q, core, tile_of(y, z)].astype(F32) + st[4][q].astype(F32)

    def z_back(st, q):
        at = st[5].at[q, core, tile_of(y, z)]
        return [send(at, at, to_z[d]) for d in (1, 2, 3)]

    def forward(st, q, block, xt, target):
        at = st[5].at[q, core, piece(block, xt)]
        return send(at, at, target)

    loads[0].wait()
    loads[1].wait()
    cells = go.shape[0]
    root = jnp.sqrt(degree[0:1, pl.ds(pl.multiple_of(y * cells, cells), cells)].astype(F32))
    for i in range(4):
        n = cells // 4
        for h in range(2):
            z_rows = lax.dot_general(
                th[h * half : (h + 1) * half], go[i * n : (i + 1) * n], (((1,), (1,)), ((), ())),
                preferred_element_type=F32,
            )
            scaled[h, :, i * n : (i + 1) * n] = (z_rows / root[:, i * n : (i + 1) * n]).astype(BF16)

    loads[2].wait()
    own_move.wait()
    dense(tiles_own, inv_own, y)
    own = {}
    for side in (0, 1):
        xt = 1 - x if side == 0 else x
        net_part(1 - core, y, xt)
        own[side] = core_send(main, whole, y, xt)
        net_part(core, y, xt)
    core_add(main, whole, own[0], y, 1 - x)
    own_x = x_send(main, whole, y)

    loads[3].wait()
    per = wpart.shape[3]

    def weight_rows(i, carry):
        rows = sa[:, pl.ds(pl.multiple_of(i * 128, 128), 128)]
        term = lax.dot_general(rows, go[...], (((0,), (0,)), ((), ())), preferred_element_type=F32)
        term = term.astype(BF16)
        for j in range(128 // per):
            wpart[0, i // 2, (i % 2) * (128 // per) + j] = term[j * per : (j + 1) * per]
        return carry

    lax.fori_loop(0, 4, weight_rows, 0)
    w_core = {}
    for side in (0, 1):
        for block in (0, 1):
            w_core[block, side] = core_send(weight, only, block, 1 - x if side == 0 else x)
    core_add(main, whole, own[1], y, x)
    w_x = []
    for block in (0, 1):
        core_add(weight, only, w_core[block, 0], block, 1 - x)
        w_x.append(x_send(weight, only, block))
    for block in (0, 1):
        core_add(weight, only, w_core[block, 1], block, x)
    x_add(main, whole, own_x, y)
    own_z = z_send(main, whole, y)

    inv_copy.wait_recv()
    inv_move = pltpu.make_async_copy(inv_land, inv_far, local_sem.at[4])
    inv_move.start()
    inv_move.wait()
    tile_copy.wait_recv()
    dense(tiles_far, inv_far, 1 - y)
    far = {}
    chunk = [pl.ds(q, 1) for q in range(CHUNKS)]
    for side in (0, 1):
        xt = 1 - x if side == 0 else x
        net_part(1 - core, 1 - y, xt)
        far[side] = [core_send(main, q, 1 - y, xt) for q in chunk]
        net_part(core, 1 - y, xt)
    w_z = []
    for block in (0, 1):
        x_add(weight, only, w_x[block], block)
        w_z.append(z_send(weight, only, block))

    pin_row = pins[0:1, pl.ds(pl.multiple_of((x * 4 + z) * tile_len, tile_len), tile_len)].astype(F32)
    row_block = 256

    def cell_sum(h, pieces, start=False, last=False):
        def rows(r, carry):
            at = pl.ds(pl.multiple_of(r * row_block, row_block), row_block)
            total = None if start else cells_sum[h, at, :]
            for block, xt in pieces:
                for p in range(2):
                    j = block * 4 + xt * 2 + p
                    net_rows = jnp.concatenate(
                        [
                            jnp.concatenate([grads[q, h, 2 * j], grads[q, h, 2 * j + 1]], axis=1)
                            for q in range(CHUNKS)
                        ],
                        axis=0,
                    )
                    term = lax.dot_general(
                        inc[j, at, :], net_rows, (((1,), (1,)), ((), ())), preferred_element_type=F32
                    )
                    total = term if total is None else total + term
            if not last:
                cells_sum[h, at, :] = total
                return carry
            for i in range(row_block // 128):
                first_row = y * cells + r * row_block + i * 128
                root_row = jnp.sqrt(
                    degree[0:1, pl.ds(pl.multiple_of(first_row, 128), 128)].astype(F32)
                )
                root_tile = jnp.broadcast_to(root_row, (128, 128)).T
                out_at = pl.ds(pl.multiple_of(r * row_block + i * 128, 128), 128)
                for w in range(half // 128):
                    out_cells[out_at, pl.ds(pl.multiple_of(h * half + w * 128, 128), 128)] = (
                        total[i * 128 : (i + 1) * 128, w * 128 : (w + 1) * 128] / root_tile
                    ).astype(BF16)
            return carry

        lax.fori_loop(0, cells // row_block, rows, 0)

    steps = []

    def step(when):
        def put(run):
            steps.append((when, len(steps), run))
            return run

        return put

    def gather_steps(st, q, start, gap, z_copies):
        got = {}

        @step(start)
        def _():
            for copy in z_copies():
                copy.wait_recv()
            got["x"] = forward(st, q, y, x, to_x)
            got["y"] = forward(st, q, y, x, to_y)
            got["core"] = [forward(st, q, y, x, to_core)]

        @step(start + gap)
        def _():
            got["x"].wait_recv()
            got["diagonal"] = forward(st, q, y, 1 - x, to_y)
            got["core"].append(forward(st, q, y, 1 - x, to_core))
            got["y"].wait_recv()
            got["core"].append(forward(st, q, 1 - y, x, to_core))

        @step(start + 2 * gap)
        def _():
            got["diagonal"].wait_recv()
            got["core"].append(forward(st, q, 1 - y, 1 - x, to_core))

        return got

    def chunk_steps(q, start, gap):
        state = {}

        @step(0)
        def _():
            core_add(main, chunk[q], far[0][q], 1 - y, 1 - x)
            state["x"] = x_send(main, chunk[q], 1 - y)

        @step(start + 0.5 * gap)
        def _():
            core_add(main, chunk[q], far[1][q], 1 - y, x)

        @step(start + gap)
        def _():
            x_add(main, chunk[q], state["x"], 1 - y)
            state["z"] = z_send(main, chunk[q], 1 - y)

        @step(start + 2 * gap)
        def _():
            z_add(main, chunk[q], state["z"], 1 - y)
            state["y"] = y_send(main, chunk[q])

        @step(start + 3 * gap)
        def _():
            total = y_total(main, chunk[q], state["y"])
            grads[chunk[q], core, tile_of(y, z)] = (total / pin_row).astype(BF16)
            state["back"] = z_back(main, chunk[q])

        return gather_steps(main, chunk[q], start + 4 * gap, gap, lambda: state["back"])

    gap = 2.0
    got = [chunk_steps(q, q * 1.0, gap) for q in range(CHUNKS)]
    w_state = {}

    @step(0.5 * gap + 0.1)
    def _():
        for block in (0, 1):
            z_add(weight, only, w_z[block], block)
        w_state["y"] = y_send(weight, only)

    @step(1.5 * gap)
    def _():
        z_add(main, whole, own_z, y)

    @step(2 * gap - 0.1)
    def _():
        total = y_total(weight, only, w_state["y"])
        wgrads[only, core, tile_of(y, z)] = total.astype(BF16)
        w_state["back"] = z_back(weight, only)

    w_got = gather_steps(weight, only, 3 * gap + 0.1, 1.5 * gap, lambda: w_state["back"])
    late = 4 * gap + CHUNKS - 1

    @step(late + 0.1)
    def _():
        cell_sum(core, [(y, x)], start=True)

    @step(late + gap + 0.1)
    def _():
        for q in range(CHUNKS):
            got[q]["core"][0].wait_recv()
        cell_sum(1 - core, [(y, x)], start=True)
        cell_sum(core, [(1 - y, x), (y, 1 - x)])

    for _, _, run in sorted(steps, key=lambda entry: entry[:2]):
        run()

    for q in range(CHUNKS):
        got[q]["core"][1].wait_recv()
        got[q]["core"][2].wait_recv()
    cell_sum(1 - core, [(1 - y, x), (y, 1 - x)])
    cell_sum(core, [(1 - y, 1 - x)], last=True)
    for copy in w_got["core"]:
        copy.wait_recv()
    for t in range(32):
        out_weight[t * per : (t + 1) * per, :] = wgrads[0, t // 16, t % 16]
    for q in range(CHUNKS):
        got[q]["core"][3].wait_recv()
    cell_sum(1 - core, [(1 - y, 1 - x)], last=True)
    for copy in copies:
        copy.wait_send()


def fused_shards(
    grad_out, saved_agg, theta, tile_values, tile_coords, block_tile_count, cell_degree, net_pin_count
):
    rows, width = grad_out.shape
    slots, tile_len = tile_values.shape[2], tile_values.shape[3]
    nets = net_pin_count.shape[0]
    net_tiles = nets // tile_len
    half, row_len = width // 2, width // 2 // CHUNKS
    per = width // 32
    vmem = pltpu.VMEM
    any_spec = pl.BlockSpec(memory_space=pl.ANY)
    vmem_spec = pl.BlockSpec(memory_space=pltpu.VMEM)

    def stage_buffers(lead, block):
        return [
            vmem(lead + (2, 16) + block, BF16),
            vmem(lead + (16,) + block, BF16),
            vmem(lead + (2, 4) + block, BF16),
            vmem(lead + (2, 3) + block, BF16),
            vmem(lead + block, BF16),
            vmem(lead + (2, 16) + block, BF16),
        ]

    return pl.pallas_call(
        exchange_kernel,
        out_shape=(
            pltpu.VMEM((rows, width), BF16),
            pltpu.VMEM((width, width), BF16),
        ),
        in_specs=[any_spec] * 4
        + [pl.BlockSpec(memory_space=pltpu.SMEM)] * 2 + [vmem_spec] * 2,
        out_specs=(vmem_spec, vmem_spec),
        scratch_shapes=[
            vmem((rows, width), BF16),
            vmem((rows, width), BF16),
            vmem((width, width), BF16),
            vmem((slots + 1, tile_len, tile_len), BF16),
            vmem((slots + 1, tile_len, tile_len), BF16),
            vmem((8, 128), jnp.int32),
            vmem((8, 128), jnp.int32),
            pltpu.SMEM((8, 128), jnp.int32),
            pltpu.SMEM((8, 128), jnp.int32),
            vmem((net_tiles, rows, 2 * tile_len), BF16),
            vmem((2, half, rows), BF16),
            vmem((2, rows, half), F32),
        ]
        + stage_buffers((CHUNKS,), (row_len, tile_len))
        + stage_buffers((1,), (per, width))
        + [
            pltpu.SemaphoreType.DMA((8,)),
            pltpu.SemaphoreType.DMA((160,)),
            pltpu.SemaphoreType.DMA((160,)),
        ],
        compiler_params=pltpu.CompilerParams(
            collective_id=0, has_side_effects=True, vmem_limit_bytes=60 * 1024 * 1024
        ),
    )(
        grad_out, saved_agg, theta, tile_values, jnp.swapaxes(tile_coords, 2, 3), block_tile_count,
        cell_degree.reshape(1, -1), net_pin_count.reshape(1, -1),
    )


def solution(mesh):
    in_specs = (
        P(("cells", "nets"), None),
        P(("cells", "nets"), None),
        P(),
        P("cells", "nets", None, None, None),
        P("cells", "nets", None, None),
        P("cells", "nets"),
        P("cells"),
        P("nets"),
    )
    fused = mesh.shape["cells"] == 16 and mesh.shape["nets"] == 2
    out_specs = (P(("cells", "nets"), None), P())
    return jax.shard_map(
        fused_shards if fused else shards, mesh=mesh, in_specs=in_specs, out_specs=out_specs, check_vma=False,
    )
```

```python
import functools

import jax
import jax.numpy as jnp
from jax import lax
from jax.experimental import pallas as pl
from jax.experimental.pallas import tpu as pltpu
from jax.sharding import PartitionSpec as P

TBLK = 16
CHUNKS = 2
F32 = jnp.float32
BF16 = jnp.bfloat16
MESH = pl.DeviceIdType.MESH


def spread_nets(tile_vals, coords, live_mask, cell_tiles, net_count):
    tile_len = tile_vals.shape[-1]
    feature_dim = cell_tiles.shape[-1]
    running = jnp.zeros((net_count, tile_len, feature_dim), jnp.float32)
    selected_tiles = cell_tiles[coords[0:TBLK, 0]]
    matrix_product = jnp.einsum(
        "cnr,cnw->crw", tile_vals, selected_tiles, preferred_element_type=jnp.float32
    )
    weight = live_mask.astype(jnp.float32)[:, None, None]
    running = running.at[coords[0:TBLK, 1]].add(matrix_product * weight)
    return running


def spread_cells(tile_vals, coords, live_mask, net_tiles, number_of_cells):
    tile_len = tile_vals.shape[-1]
    feature_dim = net_tiles.shape[-1]
    running = jnp.zeros((number_of_cells, tile_len, feature_dim), jnp.float32)
    selected_tiles = net_tiles[coords[0:TBLK, 1]]
    matrix_product = jnp.einsum(
        "jaf,jfw->jaw", tile_vals, selected_tiles, preferred_element_type=jnp.float32
    )
    weight = live_mask.astype(jnp.float32)[:, None, None]
    running = running.at[coords[0:TBLK, 0]].add(matrix_product * weight)
    return running


def shards(
    grad_out,
    saved_agg,
    theta,
    tile_values,
    tile_coords,
    block_tile_count,
    cell_degree,
    net_pin_count,
):
    own_rows = grad_out.shape[0]
    feature_dim = grad_out.shape[1]
    net_position = lax.axis_index("nets")
    cell_position = lax.axis_index("cells")
    own_degree = lax.dynamic_slice_in_dim(cell_degree, net_position * own_rows, own_rows)
    own_root = jnp.sqrt(own_degree.astype(jnp.float32))[:, None]
    grad_z = lax.dot_general(
        grad_out, theta, (((1,), (1,)), ((), ())), preferred_element_type=jnp.float32
    )
    scaled = (grad_z / own_root).astype(jnp.bfloat16)
    gathered = lax.all_gather(scaled, "nets", axis=0, tiled=True)
    theta_term = lax.dot_general(
        saved_agg, grad_out, (((0,), (0,)), ((), ())), preferred_element_type=jnp.float32
    )
    layer_weight_gradient = lax.psum(theta_term, ("cells", "nets")).astype(jnp.bfloat16)
    tile_vals = tile_values[0, 0]
    coords = tile_coords[0, 0]
    live_mask = jnp.arange(tile_vals.shape[0], dtype=jnp.int32) < block_tile_count[0, 0]
    block_cells = gathered.shape[0]
    block_nets = net_pin_count.shape[0]
    tile_len = tile_vals.shape[-1]
    number_of_cells = block_cells // tile_len
    net_count = block_nets // tile_len
    cell_tiles = gathered.reshape(number_of_cells, tile_len, feature_dim)
    net_partial = spread_nets(tile_vals, coords, live_mask, cell_tiles, net_count).reshape(
        block_nets, feature_dim
    )
    net_share = lax.psum_scatter(net_partial, "cells", scatter_dimension=0, tiled=True)
    share_rows = net_share.shape[0]
    share_degree = lax.dynamic_slice_in_dim(net_pin_count, cell_position * share_rows, share_rows)
    gradient_share = (net_share / share_degree.astype(jnp.float32)[:, None]).astype(jnp.bfloat16)
    net_grad = lax.all_gather(gradient_share, "cells", axis=0, tiled=True)
    net_tiles = net_grad.reshape(net_count, tile_len, feature_dim)
    cell_partial = spread_cells(tile_vals, coords, live_mask, net_tiles, number_of_cells).reshape(
        block_cells, feature_dim
    )
    cell_total = lax.psum_scatter(
        cell_partial.astype(jnp.bfloat16), "nets", scatter_dimension=0, tiled=True
    ).astype(jnp.float32)
    grad_cells = (cell_total / own_root).astype(jnp.bfloat16)
    return (grad_cells, layer_weight_gradient)


def exchange_kernel(
    grad_out, saved_agg, theta, tile_values, coords, live, degree, pins,
    out_cells, out_weight,
    go, sa, th, tiles_own, tiles_far, inv_vec, inv_land, inv_own, inv_far, inc, scaled, cells_sum,
    part, part_core, part_x, part_z, part_y, grads,
    wpart, wpart_core, wpart_x, wpart_z, wpart_y, wgrads,
    local_sem, send_sem, recv_sem,
):
    cell = lax.axis_index("cells")
    y = lax.axis_index("nets")
    z, x, core = cell // 4, (cell // 2) % 2, cell % 2

    def device(zt, xt, ct, yt):
        return ((zt * 2 + xt) * 2 + ct, yt)

    to_core = device(z, x, 1 - core, y)
    to_x = device(z, 1 - x, core, y)
    to_y = device(z, x, core, 1 - y)
    z_of = [lax.rem(z + d, 4) for d in range(4)]
    to_z = [device(z_of[d], x, core, y) for d in range(4)]

    loads = [
        pltpu.make_async_copy(src, dst, local_sem.at[i])
        for i, (src, dst) in enumerate(
            ((theta, th), (grad_out, go), (tile_values.at[0, 0], tiles_own.at[pl.ds(0, 16)]), (saved_agg, sa))
        )
    ]
    for load in loads:
        load.start()

    barrier = pltpu.get_barrier_semaphore()
    partners = [to_core, to_x, to_y, to_z[1], to_z[2], to_z[3]]
    for partner in partners:
        pl.semaphore_signal(barrier, inc=1, device_id=partner, device_id_type=MESH)
    pl.semaphore_wait(barrier, len(partners))

    copies = []

    def send(src, dst, target):
        i = len(copies)
        copy = pltpu.make_async_remote_copy(
            src_ref=src, dst_ref=dst, send_sem=send_sem.at[i], recv_sem=recv_sem.at[i],
            device_id=target, device_id_type=MESH,
        )
        copy.start()
        copies.append(copy)
        return copy

    tile_copy = send(tile_values.at[0, 0], tiles_far.at[pl.ds(0, 16)], to_y)
    place = lax.broadcasted_iota(jnp.int32, (8, 128), 1)
    slots = jnp.full((8, 128), 16, jnp.int32)
    for t in range(16):
        code = coords[0, 0, 0, t] * 8 + coords[0, 0, 1, t]
        code = jnp.where(t < live[0, 0], code, -1)
        slots = jnp.where(place == code, t, slots)
    inv_vec[...] = slots
    inv_copy = send(inv_vec, inv_land, to_y)
    own_move = pltpu.make_async_copy(inv_vec, inv_own, local_sem.at[5])
    own_move.start()

    tile_len = tiles_own.shape[-1]
    zero_tile = jnp.zeros((tile_len, tile_len), BF16)
    tiles_own[16] = zero_tile
    tiles_far[16] = zero_tile

    def dense(tiles, inv, block):
        def row(r, carry):
            for j in range(8):
                slot = inv[0, (y * 8 + r) * 8 + j]
                inc[
                    block * 4 + j // 2,
                    pl.ds(pl.multiple_of(r * tile_len, tile_len), tile_len),
                    (j % 2) * tile_len : (j % 2 + 1) * tile_len,
                ] = tiles[slot]
            return carry

        lax.fori_loop(0, 8, row, 0)

    half = scaled.shape[1]
    row_len = part.shape[3]

    def net_part(h, block, xt):
        def pair(p, carry):
            j = block * 4 + xt * 2 + p
            product = jnp.dot(scaled[h], inc[j], preferred_element_type=F32).astype(BF16)
            for q in range(CHUNKS):
                for s in range(2):
                    part[q, h, j * 2 + s] = product[
                        q * row_len : (q + 1) * row_len, s * tile_len : (s + 1) * tile_len
                    ]
            return carry

        lax.fori_loop(0, 2, pair, 0)

    def add(a, b):
        return (a.astype(F32) + b.astype(F32)).astype(BF16)

    def piece(block, xt):
        return pl.ds(block * 8 + xt * 4, 4)

    main = (part, part_core, part_x, part_z, part_y, grads)
    weight = (wpart, wpart_core, wpart_x, wpart_z, wpart_y, wgrads)
    whole, only = pl.ds(0, CHUNKS), pl.ds(0, 1)

    def core_send(st, q, block, xt):
        return send(st[0].at[q, 1 - core, piece(block, xt)], st[1].at[q, piece(block, xt)], to_core)

    def core_add(st, q, copy, block, xt):
        copy.wait_recv()
        at = piece(block, xt)
        st[0][q, core, at] = add(st[0][q, core, at], st[1][q, at])

    def x_send(st, q, block):
        return send(st[0].at[q, core, piece(block, 1 - x)], st[2].at[q, block], to_x)

    def x_add(st, q, copy, block):
        copy.wait_recv()
        at = piece(block, x)
        st[0][q, core, at] = add(st[0][q, core, at], st[2][q, block])

    def tile_of(block, zt):
        return block * 8 + x * 4 + zt

    def z_send(st, q, block):
        return [
            send(st[0].at[q, core, tile_of(block, z_of[d])], st[3].at[q, block, d - 1], to_z[d])
            for d in (1, 2, 3)
        ]

    def z_add(st, q, zs, block):
        total = st[0][q, core, tile_of(block, z)].astype(F32)
        for d in (1, 2, 3):
            zs[d - 1].wait_recv()
            total = total + st[3][q, block, d - 1].astype(F32)
        st[0][q, core, tile_of(block, z)] = total.astype(BF16)

    def y_send(st, q):
        return send(st[0].at[q, core, tile_of(1 - y, z)], st[4].at[q], to_y)

    def y_total(st, q, copy):
        copy.wait_recv()
        return st[0][q, core, tile_of(y, z)].astype(F32) + st[4][q].astype(F32)

    def z_back(st, q):
        at = st[5].at[q, core, tile_of(y, z)]
        return [send(at, at, to_z[d]) for d in (1, 2, 3)]

    def forward(st, q, block, xt, target):
        at = st[5].at[q, core, piece(block, xt)]
        return send(at, at, target)

    loads[0].wait()
    loads[1].wait()
    cells = go.shape[0]
    root = jnp.sqrt(degree[0:1, pl.ds(pl.multiple_of(y * cells, cells), cells)].astype(F32))
    for i in range(4):
        n = cells // 4
        for h in range(2):
            z_rows = lax.dot_general(
                th[h * half : (h + 1) * half], go[i * n : (i + 1) * n], (((1,), (1,)), ((), ())),
                preferred_element_type=F32,
            )
            scaled[h, :, i * n : (i + 1) * n] = (z_rows / root[:, i * n : (i + 1) * n]).astype(BF16)

    loads[2].wait()
    own_move.wait()
    dense(tiles_own, inv_own, y)
    own = {}
    for side in (0, 1):
        xt = 1 - x if side == 0 else x
        net_part(1 - core, y, xt)
        own[side] = core_send(main, whole, y, xt)
        if side == 1:
            core_add(main, whole, own[0], y, 1 - x)
            own_x = x_send(main, whole, y)
        net_part(core, y, xt)

    loads[3].wait()
    per = wpart.shape[3]

    def weight_rows(i, carry):
        rows = sa[:, pl.ds(pl.multiple_of(i * 128, 128), 128)]
        term = lax.dot_general(rows, go[...], (((0,), (0,)), ((), ())), preferred_element_type=F32)
        term = term.astype(BF16)
        for j in range(128 // per):
            wpart[0, i // 2, (i % 2) * (128 // per) + j] = term[j * per : (j + 1) * per]
        return carry

    lax.fori_loop(0, 4, weight_rows, 0)
    w_core = {}
    for side in (0, 1):
        for block in (0, 1):
            w_core[block, side] = core_send(weight, only, block, 1 - x if side == 0 else x)
    core_add(main, whole, own[1], y, x)
    w_x = []
    for block in (0, 1):
        core_add(weight, only, w_core[block, 0], block, 1 - x)
        w_x.append(x_send(weight, only, block))
    for block in (0, 1):
        core_add(weight, only, w_core[block, 1], block, x)

    inv_copy.wait_recv()
    inv_move = pltpu.make_async_copy(inv_land, inv_far, local_sem.at[4])
    inv_move.start()
    inv_move.wait()
    tile_copy.wait_recv()
    dense(tiles_far, inv_far, 1 - y)
    far, far_x = {}, []
    chunk = [pl.ds(q, 1) for q in range(CHUNKS)]
    for side in (0, 1):
        xt = 1 - x if side == 0 else x
        net_part(1 - core, 1 - y, xt)
        far[side] = [core_send(main, q, 1 - y, xt) for q in chunk]
        if side == 1:
            for i, q in enumerate(chunk):
                core_add(main, q, far[0][i], 1 - y, 1 - x)
                far_x.append(x_send(main, q, 1 - y))
        net_part(core, 1 - y, xt)
    x_add(main, whole, own_x, y)
    own_z = z_send(main, whole, y)
    w_z = []
    for block in (0, 1):
        x_add(weight, only, w_x[block], block)
        w_z.append(z_send(weight, only, block))

    pin_row = pins[0:1, pl.ds(pl.multiple_of((x * 4 + z) * tile_len, tile_len), tile_len)].astype(F32)
    row_block = 256

    def cell_sum(h, pieces, start=False, last=False):
        def rows(r, carry):
            at = pl.ds(pl.multiple_of(r * row_block, row_block), row_block)
            total = None if start else cells_sum[h, at, :]
            for block, xt in pieces:
                for p in range(2):
                    j = block * 4 + xt * 2 + p
                    net_rows = jnp.concatenate(
                        [
                            jnp.concatenate([grads[q, h, 2 * j], grads[q, h, 2 * j + 1]], axis=1)
                            for q in range(CHUNKS)
                        ],
                        axis=0,
                    )
                    term = lax.dot_general(
                        inc[j, at, :], net_rows, (((1,), (1,)), ((), ())), preferred_element_type=F32
                    )
                    total = term if total is None else total + term
            if not last:
                cells_sum[h, at, :] = total
                return carry
            for i in range(row_block // 128):
                first_row = y * cells + r * row_block + i * 128
                root_row = jnp.sqrt(
                    degree[0:1, pl.ds(pl.multiple_of(first_row, 128), 128)].astype(F32)
                )
                root_tile = jnp.broadcast_to(root_row, (128, 128)).T
                out_at = pl.ds(pl.multiple_of(r * row_block + i * 128, 128), 128)
                for w in range(half // 128):
                    out_cells[out_at, pl.ds(pl.multiple_of(h * half + w * 128, 128), 128)] = (
                        total[i * 128 : (i + 1) * 128, w * 128 : (w + 1) * 128] / root_tile
                    ).astype(BF16)
            return carry

        lax.fori_loop(0, cells // row_block, rows, 0)

    steps = []

    def step(when):
        def put(run):
            steps.append((when, len(steps), run))
            return run

        return put

    def gather_steps(st, q, start, gap, z_copies):
        got = {}

        @step(start)
        def _():
            for copy in z_copies():
                copy.wait_recv()
            got["x"] = forward(st, q, y, x, to_x)
            got["y"] = forward(st, q, y, x, to_y)
            got["core"] = [forward(st, q, y, x, to_core)]

        @step(start + gap)
        def _():
            got["x"].wait_recv()
            got["diagonal"] = forward(st, q, y, 1 - x, to_y)
            got["core"].append(forward(st, q, y, 1 - x, to_core))
            got["y"].wait_recv()
            got["core"].append(forward(st, q, 1 - y, x, to_core))

        @step(start + 2 * gap)
        def _():
            got["diagonal"].wait_recv()
            got["core"].append(forward(st, q, 1 - y, 1 - x, to_core))

        return got

    def chunk_steps(q, start, gap):
        state = {}

        @step(start + 0.5 * gap)
        def _():
            core_add(main, chunk[q], far[1][q], 1 - y, x)

        @step(start + gap)
        def _():
            x_add(main, chunk[q], far_x[q], 1 - y)
            state["z"] = z_send(main, chunk[q], 1 - y)

        @step(start + 2 * gap)
        def _():
            z_add(main, chunk[q], state["z"], 1 - y)
            state["y"] = y_send(main, chunk[q])

        @step(start + 3 * gap)
        def _():
            total = y_total(main, chunk[q], state["y"])
            grads[chunk[q], core, tile_of(y, z)] = (total / pin_row).astype(BF16)
            state["back"] = z_back(main, chunk[q])

        return gather_steps(main, chunk[q], start + 4 * gap, gap, lambda: state["back"])

    gap = 2.0
    got = [chunk_steps(q, q * 1.0, gap) for q in range(CHUNKS)]
    w_state = {}

    @step(0.5 * gap + 0.1)
    def _():
        for block in (0, 1):
            z_add(weight, only, w_z[block], block)
        w_state["y"] = y_send(weight, only)

    @step(1.5 * gap)
    def _():
        z_add(main, whole, own_z, y)

    @step(2 * gap - 0.1)
    def _():
        total = y_total(weight, only, w_state["y"])
        wgrads[only, core, tile_of(y, z)] = total.astype(BF16)
        w_state["back"] = z_back(weight, only)

    w_got = gather_steps(weight, only, 3 * gap + 0.1, 1.5 * gap, lambda: w_state["back"])
    late = 4 * gap + CHUNKS - 1

    @step(late + 0.1)
    def _():
        cell_sum(core, [(y, x)], start=True)

    @step(late + gap + 0.1)
    def _():
        for q in range(CHUNKS):
            got[q]["core"][0].wait_recv()
        cell_sum(1 - core, [(y, x)], start=True)
        cell_sum(core, [(1 - y, x), (y, 1 - x)])

    for _, _, run in sorted(steps, key=lambda entry: entry[:2]):
        run()

    for q in range(CHUNKS):
        got[q]["core"][1].wait_recv()
        got[q]["core"][2].wait_recv()
    cell_sum(1 - core, [(1 - y, x), (y, 1 - x)])
    cell_sum(core, [(1 - y, 1 - x)], last=True)
    for copy in w_got["core"]:
        copy.wait_recv()
    for t in range(32):
        out_weight[t * per : (t + 1) * per, :] = wgrads[0, t // 16, t % 16]
    for q in range(CHUNKS):
        got[q]["core"][3].wait_recv()
    cell_sum(1 - core, [(1 - y, 1 - x)], last=True)
    for copy in copies:
        copy.wait_send()


def fused_shards(
    grad_out, saved_agg, theta, tile_values, tile_coords, block_tile_count, cell_degree, net_pin_count
):
    rows, width = grad_out.shape
    slots, tile_len = tile_values.shape[2], tile_values.shape[3]
    nets = net_pin_count.shape[0]
    net_tiles = nets // tile_len
    half, row_len = width // 2, width // 2 // CHUNKS
    per = width // 32
    vmem = pltpu.VMEM
    any_spec = pl.BlockSpec(memory_space=pl.ANY)
    vmem_spec = pl.BlockSpec(memory_space=pltpu.VMEM)

    def stage_buffers(lead, block):
        return [
            vmem(lead + (2, 16) + block, BF16),
            vmem(lead + (16,) + block, BF16),
            vmem(lead + (2, 4) + block, BF16),
            vmem(lead + (2, 3) + block, BF16),
            vmem(lead + block, BF16),
            vmem(lead + (2, 16) + block, BF16),
        ]

    return pl.pallas_call(
        exchange_kernel,
        out_shape=(
            pltpu.VMEM((rows, width), BF16),
            pltpu.VMEM((width, width), BF16),
        ),
        in_specs=[any_spec] * 4
        + [pl.BlockSpec(memory_space=pltpu.SMEM)] * 2 + [vmem_spec] * 2,
        out_specs=(vmem_spec, vmem_spec),
        scratch_shapes=[
            vmem((rows, width), BF16),
            vmem((rows, width), BF16),
            vmem((width, width), BF16),
            vmem((slots + 1, tile_len, tile_len), BF16),
            vmem((slots + 1, tile_len, tile_len), BF16),
            vmem((8, 128), jnp.int32),
            vmem((8, 128), jnp.int32),
            pltpu.SMEM((8, 128), jnp.int32),
            pltpu.SMEM((8, 128), jnp.int32),
            vmem((net_tiles, rows, 2 * tile_len), BF16),
            vmem((2, half, rows), BF16),
            vmem((2, rows, half), F32),
        ]
        + stage_buffers((CHUNKS,), (row_len, tile_len))
        + stage_buffers((1,), (per, width))
        + [
            pltpu.SemaphoreType.DMA((8,)),
            pltpu.SemaphoreType.DMA((160,)),
            pltpu.SemaphoreType.DMA((160,)),
        ],
        compiler_params=pltpu.CompilerParams(
            collective_id=0, has_side_effects=True, vmem_limit_bytes=60 * 1024 * 1024
        ),
    )(
        grad_out, saved_agg, theta, tile_values, jnp.swapaxes(tile_coords, 2, 3), block_tile_count,
        cell_degree.reshape(1, -1), net_pin_count.reshape(1, -1),
    )


def solution(mesh):
    in_specs = (
        P(("cells", "nets"), None),
        P(("cells", "nets"), None),
        P(),
        P("cells", "nets", None, None, None),
        P("cells", "nets", None, None),
        P("cells", "nets"),
        P("cells"),
        P("nets"),
    )
    fused = mesh.shape["cells"] == 16 and mesh.shape["nets"] == 2
    out_specs = (P(("cells", "nets"), None), P())
    return jax.shard_map(
        fused_shards if fused else shards, mesh=mesh, in_specs=in_specs, out_specs=out_specs, check_vma=False,
    )
```

```python
import functools

import jax
import jax.numpy as jnp
from jax import lax
from jax.experimental import pallas as pl
from jax.experimental.pallas import tpu as pltpu
from jax.sharding import PartitionSpec as P

TBLK = 16
CHUNKS = 2
F32 = jnp.float32
BF16 = jnp.bfloat16
MESH = pl.DeviceIdType.MESH


def spread_nets(tile_vals, coords, live_mask, cell_tiles, net_count):
    tile_len = tile_vals.shape[-1]
    feature_dim = cell_tiles.shape[-1]
    running = jnp.zeros((net_count, tile_len, feature_dim), jnp.float32)
    selected_tiles = cell_tiles[coords[0:TBLK, 0]]
    matrix_product = jnp.einsum(
        "cnr,cnw->crw", tile_vals, selected_tiles, preferred_element_type=jnp.float32
    )
    weight = live_mask.astype(jnp.float32)[:, None, None]
    running = running.at[coords[0:TBLK, 1]].add(matrix_product * weight)
    return running


def spread_cells(tile_vals, coords, live_mask, net_tiles, number_of_cells):
    tile_len = tile_vals.shape[-1]
    feature_dim = net_tiles.shape[-1]
    running = jnp.zeros((number_of_cells, tile_len, feature_dim), jnp.float32)
    selected_tiles = net_tiles[coords[0:TBLK, 1]]
    matrix_product = jnp.einsum(
        "jaf,jfw->jaw", tile_vals, selected_tiles, preferred_element_type=jnp.float32
    )
    weight = live_mask.astype(jnp.float32)[:, None, None]
    running = running.at[coords[0:TBLK, 0]].add(matrix_product * weight)
    return running


def shards(
    grad_out,
    saved_agg,
    theta,
    tile_values,
    tile_coords,
    block_tile_count,
    cell_degree,
    net_pin_count,
):
    own_rows = grad_out.shape[0]
    feature_dim = grad_out.shape[1]
    net_position = lax.axis_index("nets")
    cell_position = lax.axis_index("cells")
    own_degree = lax.dynamic_slice_in_dim(cell_degree, net_position * own_rows, own_rows)
    own_root = jnp.sqrt(own_degree.astype(jnp.float32))[:, None]
    grad_z = lax.dot_general(
        grad_out, theta, (((1,), (1,)), ((), ())), preferred_element_type=jnp.float32
    )
    scaled = (grad_z / own_root).astype(jnp.bfloat16)
    gathered = lax.all_gather(scaled, "nets", axis=0, tiled=True)
    theta_term = lax.dot_general(
        saved_agg, grad_out, (((0,), (0,)), ((), ())), preferred_element_type=jnp.float32
    )
    layer_weight_gradient = lax.psum(theta_term, ("cells", "nets")).astype(jnp.bfloat16)
    tile_vals = tile_values[0, 0]
    coords = tile_coords[0, 0]
    live_mask = jnp.arange(tile_vals.shape[0], dtype=jnp.int32) < block_tile_count[0, 0]
    block_cells = gathered.shape[0]
    block_nets = net_pin_count.shape[0]
    tile_len = tile_vals.shape[-1]
    number_of_cells = block_cells // tile_len
    net_count = block_nets // tile_len
    cell_tiles = gathered.reshape(number_of_cells, tile_len, feature_dim)
    net_partial = spread_nets(tile_vals, coords, live_mask, cell_tiles, net_count).reshape(
        block_nets, feature_dim
    )
    net_share = lax.psum_scatter(net_partial, "cells", scatter_dimension=0, tiled=True)
    share_rows = net_share.shape[0]
    share_degree = lax.dynamic_slice_in_dim(net_pin_count, cell_position * share_rows, share_rows)
    gradient_share = (net_share / share_degree.astype(jnp.float32)[:, None]).astype(jnp.bfloat16)
    net_grad = lax.all_gather(gradient_share, "cells", axis=0, tiled=True)
    net_tiles = net_grad.reshape(net_count, tile_len, feature_dim)
    cell_partial = spread_cells(tile_vals, coords, live_mask, net_tiles, number_of_cells).reshape(
        block_cells, feature_dim
    )
    cell_total = lax.psum_scatter(
        cell_partial.astype(jnp.bfloat16), "nets", scatter_dimension=0, tiled=True
    ).astype(jnp.float32)
    grad_cells = (cell_total / own_root).astype(jnp.bfloat16)
    return (grad_cells, layer_weight_gradient)


def exchange_kernel(
    grad_out, saved_agg, theta, tile_values, coords, live, degree, pins,
    out_cells, out_weight,
    go, sa, th, tiles_own, tiles_far, inv_vec, inv_land, inv_own, inv_far, inc, scaled, cells_sum,
    part, part_core, part_x, part_z, part_y, grads,
    wpart, wpart_core, wpart_x, wpart_z, wpart_y, wgrads,
    local_sem, send_sem, recv_sem,
):
    cell = lax.axis_index("cells")
    y = lax.axis_index("nets")
    z, x, core = cell // 4, (cell // 2) % 2, cell % 2

    def device(zt, xt, ct, yt):
        return ((zt * 2 + xt) * 2 + ct, yt)

    to_core = device(z, x, 1 - core, y)
    to_x = device(z, 1 - x, core, y)
    to_y = device(z, x, core, 1 - y)
    z_of = [lax.rem(z + d, 4) for d in range(4)]
    to_z = [device(z_of[d], x, core, y) for d in range(4)]

    loads = [
        pltpu.make_async_copy(src, dst, local_sem.at[i])
        for i, (src, dst) in enumerate(
            ((theta, th), (grad_out, go), (tile_values.at[0, 0], tiles_own.at[pl.ds(0, 16)]), (saved_agg, sa))
        )
    ]
    for load in loads:
        load.start()

    barrier = pltpu.get_barrier_semaphore()
    partners = [to_core, to_x, to_y, to_z[1], to_z[2], to_z[3]]
    for partner in partners:
        pl.semaphore_signal(barrier, inc=1, device_id=partner, device_id_type=MESH)
    pl.semaphore_wait(barrier, len(partners))

    copies = []

    def send(src, dst, target):
        i = len(copies)
        copy = pltpu.make_async_remote_copy(
            src_ref=src, dst_ref=dst, send_sem=send_sem.at[i], recv_sem=recv_sem.at[i],
            device_id=target, device_id_type=MESH,
        )
        copy.start()
        copies.append(copy)
        return copy

    tile_copy = send(tile_values.at[0, 0], tiles_far.at[pl.ds(0, 16)], to_y)
    place = lax.broadcasted_iota(jnp.int32, (8, 128), 1)
    slots = jnp.full((8, 128), 16, jnp.int32)
    for t in range(16):
        code = coords[0, 0, 0, t] * 8 + coords[0, 0, 1, t]
        code = jnp.where(t < live[0, 0], code, -1)
        slots = jnp.where(place == code, t, slots)
    inv_vec[...] = slots
    inv_copy = send(inv_vec, inv_land, to_y)
    own_move = pltpu.make_async_copy(inv_vec, inv_own, local_sem.at[5])
    own_move.start()

    tile_len = tiles_own.shape[-1]
    zero_tile = jnp.zeros((tile_len, tile_len), BF16)
    tiles_own[16] = zero_tile
    tiles_far[16] = zero_tile

    def dense(tiles, inv, block):
        def row(r, carry):
            for j in range(8):
                slot = inv[0, (y * 8 + r) * 8 + j]
                inc[
                    block * 4 + j // 2,
                    pl.ds(pl.multiple_of(r * tile_len, tile_len), tile_len),
                    (j % 2) * tile_len : (j % 2 + 1) * tile_len,
                ] = tiles[slot]
            return carry

        lax.fori_loop(0, 8, row, 0)

    half = scaled.shape[1]
    row_len = part.shape[3]

    def net_part(h, block, xt):
        def pair(p, carry):
            j = block * 4 + xt * 2 + p
            product = jnp.dot(scaled[h], inc[j], preferred_element_type=F32).astype(BF16)
            for q in range(CHUNKS):
                for s in range(2):
                    part[q, h, j * 2 + s] = product[
                        q * row_len : (q + 1) * row_len, s * tile_len : (s + 1) * tile_len
                    ]
            return carry

        lax.fori_loop(0, 2, pair, 0)

    def add(a, b):
        return (a.astype(F32) + b.astype(F32)).astype(BF16)

    def piece(block, xt):
        return pl.ds(block * 8 + xt * 4, 4)

    main = (part, part_core, part_x, part_z, part_y, grads)
    weight = (wpart, wpart_core, wpart_x, wpart_z, wpart_y, wgrads)
    whole, only = pl.ds(0, CHUNKS), pl.ds(0, 1)

    def core_send(st, q, block, xt):
        return send(st[0].at[q, 1 - core, piece(block, xt)], st[1].at[q, piece(block, xt)], to_core)

    def core_add(st, q, copy, block, xt):
        copy.wait_recv()
        at = piece(block, xt)
        st[0][q, core, at] = add(st[0][q, core, at], st[1][q, at])

    def x_send(st, q, block):
        return send(st[0].at[q, core, piece(block, 1 - x)], st[2].at[q, block], to_x)

    def x_add(st, q, copy, block):
        copy.wait_recv()
        at = piece(block, x)
        st[0][q, core, at] = add(st[0][q, core, at], st[2][q, block])

    def tile_of(block, zt):
        return block * 8 + x * 4 + zt

    def z_send(st, q, block):
        return [
            send(st[0].at[q, core, tile_of(block, z_of[d])], st[3].at[q, block, d - 1], to_z[d])
            for d in (1, 2, 3)
        ]

    def z_add(st, q, zs, block):
        total = st[0][q, core, tile_of(block, z)].astype(F32)
        for d in (1, 2, 3):
            zs[d - 1].wait_recv()
            total = total + st[3][q, block, d - 1].astype(F32)
        st[0][q, core, tile_of(block, z)] = total.astype(BF16)

    def y_send(st, q):
        return send(st[0].at[q, core, tile_of(1 - y, z)], st[4].at[q], to_y)

    def y_total(st, q, copy):
        copy.wait_recv()
        return st[0][q, core, tile_of(y, z)].astype(F32) + st[4][q].astype(F32)

    def z_back(st, q):
        at = st[5].at[q, core, tile_of(y, z)]
        return [send(at, at, to_z[d]) for d in (1, 2, 3)]

    def forward(st, q, block, xt, target):
        at = st[5].at[q, core, piece(block, xt)]
        return send(at, at, target)

    loads[0].wait()
    loads[1].wait()
    cells = go.shape[0]
    root = jnp.sqrt(degree[0:1, pl.ds(pl.multiple_of(y * cells, cells), cells)].astype(F32))
    for i in range(4):
        n = cells // 4
        for h in range(2):
            z_rows = lax.dot_general(
                th[h * half : (h + 1) * half], go[i * n : (i + 1) * n], (((1,), (1,)), ((), ())),
                preferred_element_type=F32,
            )
            scaled[h, :, i * n : (i + 1) * n] = (z_rows / root[:, i * n : (i + 1) * n]).astype(BF16)

    loads[2].wait()
    own_move.wait()
    dense(tiles_own, inv_own, y)
    own = {}
    for side in (0, 1):
        xt = 1 - x if side == 0 else x
        net_part(1 - core, y, xt)
        own[side] = core_send(main, whole, y, xt)
        if side == 1:
            core_add(main, whole, own[0], y, 1 - x)
            own_x = x_send(main, whole, y)
        net_part(core, y, xt)

    loads[3].wait()
    per = wpart.shape[3]

    def weight_rows(i, carry):
        rows = sa[:, pl.ds(pl.multiple_of(i * 128, 128), 128)]
        term = lax.dot_general(rows, go[...], (((0,), (0,)), ((), ())), preferred_element_type=F32)
        term = term.astype(BF16)
        for j in range(128 // per):
            wpart[0, i // 2, (i % 2) * (128 // per) + j] = term[j * per : (j + 1) * per]
        return carry

    lax.fori_loop(0, 4, weight_rows, 0)
    w_core = {}
    for side in (0, 1):
        for block in (0, 1):
            w_core[block, side] = core_send(weight, only, block, 1 - x if side == 0 else x)
    core_add(main, whole, own[1], y, x)
    w_x = []
    for block in (0, 1):
        core_add(weight, only, w_core[block, 0], block, 1 - x)
        w_x.append(x_send(weight, only, block))
    for block in (0, 1):
        core_add(weight, only, w_core[block, 1], block, x)

    x_add(main, whole, own_x, y)
    own_z = z_send(main, whole, y)

    inv_copy.wait_recv()
    inv_move = pltpu.make_async_copy(inv_land, inv_far, local_sem.at[4])
    inv_move.start()
    inv_move.wait()
    tile_copy.wait_recv()
    dense(tiles_far, inv_far, 1 - y)
    far, far_x = {}, []
    chunk = [pl.ds(q, 1) for q in range(CHUNKS)]
    for side in (0, 1):
        xt = 1 - x if side == 0 else x
        net_part(1 - core, 1 - y, xt)
        far[side] = [core_send(main, q, 1 - y, xt) for q in chunk]
        if side == 1:
            for i, q in enumerate(chunk):
                core_add(main, q, far[0][i], 1 - y, 1 - x)
                far_x.append(x_send(main, q, 1 - y))
        net_part(core, 1 - y, xt)
    w_z = []
    for block in (0, 1):
        x_add(weight, only, w_x[block], block)
        w_z.append(z_send(weight, only, block))

    pin_row = pins[0:1, pl.ds(pl.multiple_of((x * 4 + z) * tile_len, tile_len), tile_len)].astype(F32)
    row_block = 256

    def cell_sum(h, pieces, start=False, last=False):
        def rows(r, carry):
            at = pl.ds(pl.multiple_of(r * row_block, row_block), row_block)
            total = None if start else cells_sum[h, at, :]
            for block, xt in pieces:
                for p in range(2):
                    j = block * 4 + xt * 2 + p
                    net_rows = jnp.concatenate(
                        [
                            jnp.concatenate([grads[q, h, 2 * j], grads[q, h, 2 * j + 1]], axis=1)
                            for q in range(CHUNKS)
                        ],
                        axis=0,
                    )
                    term = lax.dot_general(
                        inc[j, at, :], net_rows, (((1,), (1,)), ((), ())), preferred_element_type=F32
                    )
                    total = term if total is None else total + term
            if not last:
                cells_sum[h, at, :] = total
                return carry
            for i in range(row_block // 128):
                first_row = y * cells + r * row_block + i * 128
                root_row = jnp.sqrt(
                    degree[0:1, pl.ds(pl.multiple_of(first_row, 128), 128)].astype(F32)
                )
                root_tile = jnp.broadcast_to(root_row, (128, 128)).T
                out_at = pl.ds(pl.multiple_of(r * row_block + i * 128, 128), 128)
                for w in range(half // 128):
                    out_cells[out_at, pl.ds(pl.multiple_of(h * half + w * 128, 128), 128)] = (
                        total[i * 128 : (i + 1) * 128, w * 128 : (w + 1) * 128] / root_tile
                    ).astype(BF16)
            return carry

        lax.fori_loop(0, cells // row_block, rows, 0)

    steps = []

    def step(when):
        def put(run):
            steps.append((when, len(steps), run))
            return run

        return put

    def gather_steps(st, q, start, gap, z_copies):
        got = {}

        @step(start)
        def _():
            for copy in z_copies():
                copy.wait_recv()
            got["x"] = forward(st, q, y, x, to_x)
            got["y"] = forward(st, q, y, x, to_y)
            got["core"] = [forward(st, q, y, x, to_core)]

        @step(start + gap)
        def _():
            got["x"].wait_recv()
            got["diagonal"] = forward(st, q, y, 1 - x, to_y)
            got["core"].append(forward(st, q, y, 1 - x, to_core))
            got["y"].wait_recv()
            got["core"].append(forward(st, q, 1 - y, x, to_core))

        @step(start + 2 * gap)
        def _():
            got["diagonal"].wait_recv()
            got["core"].append(forward(st, q, 1 - y, 1 - x, to_core))

        return got

    def chunk_steps(q, start, gap):
        state = {}

        @step(start + 0.5 * gap)
        def _():
            core_add(main, chunk[q], far[1][q], 1 - y, x)

        @step(start + gap)
        def _():
            x_add(main, chunk[q], far_x[q], 1 - y)
            state["z"] = z_send(main, chunk[q], 1 - y)

        @step(start + 2 * gap)
        def _():
            z_add(main, chunk[q], state["z"], 1 - y)
            state["y"] = y_send(main, chunk[q])

        @step(start + 3 * gap)
        def _():
            total = y_total(main, chunk[q], state["y"])
            grads[chunk[q], core, tile_of(y, z)] = (total / pin_row).astype(BF16)
            state["back"] = z_back(main, chunk[q])

        return gather_steps(main, chunk[q], start + 4 * gap, gap, lambda: state["back"])

    gap = 2.0
    got = [chunk_steps(q, q * 1.0, gap) for q in range(CHUNKS)]
    w_state = {}

    @step(0.5 * gap + 0.1)
    def _():
        for block in (0, 1):
            z_add(weight, only, w_z[block], block)
        w_state["y"] = y_send(weight, only)

    @step(1.5 * gap)
    def _():
        z_add(main, whole, own_z, y)

    @step(2 * gap - 0.1)
    def _():
        total = y_total(weight, only, w_state["y"])
        wgrads[only, core, tile_of(y, z)] = total.astype(BF16)
        w_state["back"] = z_back(weight, only)

    w_got = gather_steps(weight, only, 3 * gap + 0.1, 1.5 * gap, lambda: w_state["back"])
    late = 4 * gap + CHUNKS - 1

    @step(late + 0.1)
    def _():
        cell_sum(core, [(y, x)], start=True)

    @step(late + gap + 0.1)
    def _():
        for q in range(CHUNKS):
            got[q]["core"][0].wait_recv()
        cell_sum(1 - core, [(y, x)], start=True)
        cell_sum(core, [(1 - y, x), (y, 1 - x)])

    for _, _, run in sorted(steps, key=lambda entry: entry[:2]):
        run()

    for q in range(CHUNKS):
        got[q]["core"][1].wait_recv()
        got[q]["core"][2].wait_recv()
    cell_sum(1 - core, [(1 - y, x), (y, 1 - x)])
    cell_sum(core, [(1 - y, 1 - x)], last=True)
    for copy in w_got["core"]:
        copy.wait_recv()
    for t in range(32):
        out_weight[t * per : (t + 1) * per, :] = wgrads[0, t // 16, t % 16]
    for q in range(CHUNKS):
        got[q]["core"][3].wait_recv()
    cell_sum(1 - core, [(1 - y, 1 - x)], last=True)
    for copy in copies:
        copy.wait_send()


def fused_shards(
    grad_out, saved_agg, theta, tile_values, tile_coords, block_tile_count, cell_degree, net_pin_count
):
    rows, width = grad_out.shape
    slots, tile_len = tile_values.shape[2], tile_values.shape[3]
    nets = net_pin_count.shape[0]
    net_tiles = nets // tile_len
    half, row_len = width // 2, width // 2 // CHUNKS
    per = width // 32
    vmem = pltpu.VMEM
    any_spec = pl.BlockSpec(memory_space=pl.ANY)
    vmem_spec = pl.BlockSpec(memory_space=pltpu.VMEM)

    def stage_buffers(lead, block):
        return [
            vmem(lead + (2, 16) + block, BF16),
            vmem(lead + (16,) + block, BF16),
            vmem(lead + (2, 4) + block, BF16),
            vmem(lead + (2, 3) + block, BF16),
            vmem(lead + block, BF16),
            vmem(lead + (2, 16) + block, BF16),
        ]

    return pl.pallas_call(
        exchange_kernel,
        out_shape=(
            pltpu.VMEM((rows, width), BF16),
            pltpu.VMEM((width, width), BF16),
        ),
        in_specs=[any_spec] * 4
        + [pl.BlockSpec(memory_space=pltpu.SMEM)] * 2 + [vmem_spec] * 2,
        out_specs=(vmem_spec, vmem_spec),
        scratch_shapes=[
            vmem((rows, width), BF16),
            vmem((rows, width), BF16),
            vmem((width, width), BF16),
            vmem((slots + 1, tile_len, tile_len), BF16),
            vmem((slots + 1, tile_len, tile_len), BF16),
            vmem((8, 128), jnp.int32),
            vmem((8, 128), jnp.int32),
            pltpu.SMEM((8, 128), jnp.int32),
            pltpu.SMEM((8, 128), jnp.int32),
            vmem((net_tiles, rows, 2 * tile_len), BF16),
            vmem((2, half, rows), BF16),
            vmem((2, rows, half), F32),
        ]
        + stage_buffers((CHUNKS,), (row_len, tile_len))
        + stage_buffers((1,), (per, width))
        + [
            pltpu.SemaphoreType.DMA((8,)),
            pltpu.SemaphoreType.DMA((160,)),
            pltpu.SemaphoreType.DMA((160,)),
        ],
        compiler_params=pltpu.CompilerParams(
            collective_id=0, has_side_effects=True, vmem_limit_bytes=60 * 1024 * 1024
        ),
    )(
        grad_out, saved_agg, theta, tile_values, jnp.swapaxes(tile_coords, 2, 3), block_tile_count,
        cell_degree.reshape(1, -1), net_pin_count.reshape(1, -1),
    )


def solution(mesh):
    in_specs = (
        P(("cells", "nets"), None),
        P(("cells", "nets"), None),
        P(),
        P("cells", "nets", None, None, None),
        P("cells", "nets", None, None),
        P("cells", "nets"),
        P("cells"),
        P("nets"),
    )
    fused = mesh.shape["cells"] == 16 and mesh.shape["nets"] == 2
    out_specs = (P(("cells", "nets"), None), P())
    return jax.shard_map(
        fused_shards if fused else shards, mesh=mesh, in_specs=in_specs, out_specs=out_specs, check_vma=False,
    )
```
